512 devices in a mesh: ens: 8 (over x, core), row: 16 (over y_hi, z), col: 4 (over y_lo).
Axes of the slice: x: 4, y: 8 (y_hi: 2, y_lo: 4; y = y_hi * 4 + y_lo), z: 8, core: 2. Of those that a mesh axis runs over, the one named last changes fastest.
Arguments:
- theta: float32 [64, 1024, 1024], P('ens', 'row', 'col'), may hold values from -1.2 to 1.2
- initial: float32 [1024, 1024], P('row', 'col'), may hold values from -6 to 6
- velocity: float32 [2, 1024, 1024], P(None, 'row', 'col'), may hold values from -4 to 4
- sensors: int32 [16, 4, 256], P('row', 'col'), may hold values from 0 to 16383
- target: float32 [16, 4, 256], P('row', 'col'), may hold values from -6 to 6
- noise: float32 [16, 4, 256], P('row', 'col'), may hold values from 0.5 to 5
Outputs:
- theta_new: float32 [64, 1024, 1024], P('ens', 'row', 'col')
- predictions: float32 [64, 16, 4, 256], P('ens', 'row', 'col')
The draws below stay inside these ranges and needn't reach their ends.
Inputs may be any that keep to these rules, and one draw needn't show every extreme that they name: `sensors`: an entry is r * 256 + c for a cell at row r and column c of the block of 64 x 256 cells of the device with those row and col indices.
All inputs are finite; a program needn't handle non-finite values.
Results may differ from the reference program's by a relative error of at most 0.0003.
Values sent between devices are 32-bit elements; how exact they have to be, the bound alone decides.
A program may use at most 64 MiB of HBM per device.

```python
import math
import jax
import jax.numpy as jnp
from jax import lax

RD = 64
CD = 256
SENS_DEV = 256
STEPS = 4
ENS = 64
NR = 1024
NC = 1024
N_ROW = 16
N_COL = 4


def with_ends(entries, own_key, least, high):
    dims = entries.shape
    place = [jax.random.randint(jax.random.fold_in(own_key, axis), (), 0, dims[axis]) for axis in range(len(dims))]
    entries = entries.at[tuple(place)].set(least)
    longest = dims.index(max(dims))
    place[longest] = (place[longest] + 1) % dims[longest]
    return entries.at[tuple(place)].set(high)


def steps_of(rng, shape, pieces, low, top_value):
    level, own = 1.0, jax.random.fold_in(rng, 6)
    for position, parts in pieces:
        draws = jnp.exp(jax.random.uniform(jax.random.fold_in(own, position), (parts,), jnp.float32, low / len(pieces), top_value / len(pieces)))
        level = level * jnp.repeat(draws, shape[position] // parts).reshape([-1 if axis == position else 1 for axis in range(len(shape))])
    return level


def bell_draw(stream_key, shape, deviation, limit, shards=(), kind=jnp.bfloat16):
    loudness = steps_of(stream_key, shape, shards, -0.22, 0.18) if shards else 1.0
    entries = jax.random.normal(stream_key, shape, jnp.float32) * deviation * loudness
    return jnp.minimum(jnp.maximum(entries, -limit), limit).astype(kind)


def setup_inputs(seed: int = 0) -> dict:
    arg_keys = jax.random.split(jax.random.key(seed), 7)
    theta = jnp.clip(jax.random.uniform(arg_keys[0], (ENS, NR, NC), jnp.float32, -1.2, 1.2) * steps_of(arg_keys[0], (ENS, NR, NC), ((0, 8), (1, 16), (2, 4)), -0.4, 0.0), -1.2, 1.2)
    initial = bell_draw(arg_keys[1], (NR, NC), 1.0, 6.0, ((0, 16), (1, 4)), jnp.float32)
    velocity = bell_draw(arg_keys[2], (2, NR, NC), 1.0, 4.0, ((1, 16), (2, 4)), jnp.float32)
    sensors = with_ends(jax.random.randint(arg_keys[3], (N_ROW, N_COL, SENS_DEV), 0, RD * CD), jax.random.fold_in(arg_keys[3], 1), 0, (RD * CD) - 1).astype(jnp.int32)
    target = bell_draw(arg_keys[4], (N_ROW, N_COL, SENS_DEV), 1.0, 6.0, ((0, 16), (1, 4)), jnp.float32)
    noise = jnp.clip(jnp.exp(math.log(5.0) - 2.3025851 * jax.random.uniform(arg_keys[5], (N_ROW, N_COL, SENS_DEV), jnp.float32) ** steps_of(arg_keys[5], (N_ROW, N_COL, SENS_DEV), ((0, 16), (1, 4)), -0.2, 0.2)), 0.5, 5.0)
    return {"theta": theta, "initial": initial, "velocity": velocity, "sensors": sensors, "target": target, "noise": noise}


diffuse_rate = 0.07
advect_rate = 0.3

def advance(state, kappa, vel_row, vel_col):
    center = state[:, 1:-1, 1:-1]
    kappa_mid = kappa[:, 1:-1, 1:-1]
    upper = state[:, 2:, 1:-1]
    lower = state[:, :-2, 1:-1]
    right_cell = state[:, 1:-1, 2:]
    left_cell = state[:, 1:-1, :-2]
    face_up = 0.5 * (kappa_mid + kappa[:, 2:, 1:-1])
    face_down = 0.5 * (kappa_mid + kappa[:, :-2, 1:-1])
    face_right = 0.5 * (kappa_mid + kappa[:, 1:-1, 2:])
    face_left = 0.5 * (kappa_mid + kappa[:, 1:-1, :-2])
    flux = face_up * (upper - center) - face_down * (center - lower) + face_right * (right_cell - center) - face_left * (center - left_cell)
    transport = vel_row[1:-1, 1:-1] * (upper - lower) + vel_col[1:-1, 1:-1] * (right_cell - left_cell)
    return center + diffuse_rate * flux - 0.5 * advect_rate * transport

def reference(theta, initial, velocity, sensors, target, noise):
    vel_row = jnp.pad(velocity[0], 1)
    vel_col = jnp.pad(velocity[1], 1)

    def forward(member_theta):
        kappa = jnp.pad(jnp.exp(member_theta), 1)[None]
        field = initial[None]
        for step_index in range(STEPS):
            field = advance(jnp.pad(field, ((0, 0), (1, 1), (1, 1))), kappa, vel_row, vel_col)
        blocks = field[0].reshape(N_ROW, RD, N_COL, CD).transpose(0, 2, 1, 3).reshape(N_ROW, N_COL, RD * CD)
        return jnp.take_along_axis(blocks, sensors, axis=2)
    predictions = lax.map(forward, theta)
    flat = predictions.reshape(predictions.shape[0], -1)
    mean_obs = jnp.mean(flat, axis=0)
    anomalies = flat - mean_obs
    weighted = anomalies / noise.reshape(-1)
    miss = target.reshape(-1) - flat
    gram = jnp.dot(weighted.astype(jnp.float32), anomalies.T.astype(jnp.float32), precision=lax.Precision.HIGHEST, preferred_element_type=jnp.float32)
    cross = jnp.dot(weighted.astype(jnp.float32), miss.T.astype(jnp.float32), precision=lax.Precision.HIGHEST, preferred_element_type=jnp.float32)
    members = flat.shape[0]
    system = jnp.eye(members, dtype=jnp.float32) + gram / (members - 1)
    factor = jnp.linalg.cholesky(system)
    mixing = jax.scipy.linalg.cho_solve((factor, True), cross) / (members - 1)
    theta_new = theta + jnp.einsum('krc,km->mrc', theta, mixing, precision=lax.Precision.HIGHEST)
    return (theta_new, predictions)
```

```python
import functools

import jax
import jax.numpy as jnp
from jax import lax
from jax.experimental import pallas as pl
from jax.experimental.pallas import tpu as pltpu
from jax.sharding import PartitionSpec as P

STEPS = 4
diffuse_rate = 0.07
advect_rate = 0.3

MESH = pl.DeviceIdType.MESH
HALO = 4
LANES = 128


def roll(x, shift, axis):
    shift = shift % x.shape[axis]
    return x if shift == 0 else pltpu.roll(x, shift, axis)


def split_bf16(x):
    hi = x.astype(jnp.bfloat16)
    lo = (x - hi.astype(jnp.float32)).astype(jnp.bfloat16)
    return hi, lo


def dot32(a, b):
    return jnp.dot(a, b, preferred_element_type=jnp.float32)


def kernel(
    sizes,
    theta, initial, velocity, sensors, target, noise,
    out, pred,
    blocks, extra, sens_v, targ_v, noise_v,
    row_send, row_recv, col_send, col_recv, corner_recv,
    ext, field, preds, zbuf, ybuf, gall, result,
    load_sem, halo_ssem, halo_rsem, pred_ssem, pred_rsem,
    z_ssem, z_rsem, y_ssem, y_rsem, g_ssem, g_rsem,
    th_ssem, th_rsem, out_sem,
):
    n_e, n_r, n_c, n_z = sizes
    n_x = n_e // 2
    n_yh = n_r // n_z
    n_y = n_yh * n_c
    mem, rows, cols = theta.shape
    rext, cext = rows + 2 * HALO, cols + LANES
    planes = mem + 3
    e, r, c = lax.axis_index("ens"), lax.axis_index("row"), lax.axis_index("col")
    x, core = e // 2, e % 2
    yh, z = r // n_z, r % n_z
    y = yh * n_c + c

    loads = [
        pltpu.make_async_copy(theta, blocks.at[e], load_sem.at[0]),
        pltpu.make_async_copy(initial, extra.at[0], load_sem.at[1]),
        pltpu.make_async_copy(velocity, extra.at[pl.ds(1, 2)], load_sem.at[2]),
        pltpu.make_async_copy(sensors, sens_v, load_sem.at[3]),
        pltpu.make_async_copy(target, targ_v, load_sem.at[4]),
        pltpu.make_async_copy(noise, noise_v, load_sem.at[5]),
    ]
    for copy in loads:
        copy.start()

    prev, nxt = (r + n_r - 1) % n_r, (r + 1) % n_r
    left, right = (c + n_c - 1) % n_c, (c + 1) % n_c
    halo_ids = [
        {"row": prev}, {"row": nxt}, {"col": left}, {"col": right},
        {"row": prev, "col": left}, {"row": prev, "col": right},
        {"row": nxt, "col": left}, {"row": nxt, "col": right},
    ]
    ens_ids = [{"ens": (e + d) % n_e} for d in range(1, n_e)]
    z_ids = [{"row": yh * n_z + (z + d) % n_z} for d in range(1, n_z)]
    y_ids = []
    for d in range(1, n_y):
        other = (y + d) % n_y
        y_ids.append({"row": (other // n_c) * n_z + z, "col": other % n_c})

    barrier = pltpu.get_barrier_semaphore()
    everyone = halo_ids + ens_ids + z_ids + y_ids
    for device in everyone:
        pl.semaphore_signal(barrier, inc=1, device_id=device, device_id_type=MESH)
    pl.semaphore_wait(barrier, len(everyone))

    sends = []

    def remote(src, dst, ssem, rsem, device):
        copy = pltpu.make_async_remote_copy(
            src_ref=src, dst_ref=dst, send_sem=ssem, recv_sem=rsem,
            device_id=device, device_id_type=MESH,
        )
        return copy

    def send(*args):
        copy = remote(*args)
        copy.start()
        sends.append(copy)
        return copy

    for copy in loads:
        copy.wait()

    half = mem // 2
    x_r, x_l, x_f = (x + 1) % n_x, (x + n_x - 1) % n_x, (x + 2) % n_x
    to_r, to_l = {"ens": x_r * 2 + core}, {"ens": x_l * 2 + core}
    to_o = {"ens": x * 2 + (1 - core)}

    def part(index, h):
        return blocks.at[index, pl.ds(h * half, half)]

    def send_half(index, h, slot, device):
        return send(part(index, h), part(index, h), th_ssem.at[slot], th_rsem.at[slot], device)

    sub = lax.broadcasted_iota(jnp.int32, (8, cols), 0)
    low_sub = sub < HALO

    def plane(p):
        return blocks.at[e, p] if p < mem else extra.at[p - mem]

    for pair in range((planes + 1) // 2):
        a, b = 2 * pair, min(2 * pair + 1, planes - 1)
        fa, fb = plane(a)[0:8, :], plane(b)[0:8, :]
        la, lb = plane(a)[rows - 8 : rows, :], plane(b)[rows - 8 : rows, :]
        row_send[0, pair] = jnp.where(low_sub, fa, roll(fb, HALO, 0))
        row_send[1, pair] = jnp.where(low_sub, roll(la, HALO, 0), lb)
    send(row_send.at[0], row_recv.at[0], halo_ssem.at[0], halo_rsem.at[0], halo_ids[0])
    send(row_send.at[1], row_recv.at[1], halo_ssem.at[1], halo_rsem.at[1], halo_ids[1])

    lane = lax.broadcasted_iota(jnp.int32, (rows, LANES), 1)
    slot_of = lane // HALO
    to_left = jnp.zeros((rows, LANES), jnp.float32)
    to_right = jnp.zeros((rows, LANES), jnp.float32)
    for p in range(planes):
        ref = plane(p)
        to_left = jnp.where(slot_of == p, roll(ref[:, 0:LANES], HALO * p, 1), to_left)
        to_right = jnp.where(
            slot_of == p, roll(ref[:, cols - LANES : cols], HALO * p + HALO, 1), to_right
        )
    col_send[0] = to_left
    col_send[1] = to_right
    send(col_send.at[0], col_recv.at[0], halo_ssem.at[2], halo_rsem.at[2], halo_ids[2])
    send(col_send.at[1], col_recv.at[1], halo_ssem.at[3], halo_rsem.at[3], halo_ids[3])
    for k in range(4):
        edge = pl.ds(0, 8) if k < 2 else pl.ds(rows - 8, 8)
        send(
            col_send.at[k % 2, edge], corner_recv.at[k],
            halo_ssem.at[4 + k], halo_rsem.at[4 + k], halo_ids[4 + k],
        )
    halo_copies = list(sends)

    for h in range(2):
        send_half(e, h, h, to_r)
        send_half(e, 1 - h, 2 + 1 - h, to_l)
    for h in range(2):
        send_half(e, h, 4 + h, to_o)

    for p in range(planes):
        ext[p, 0:rows, 0:cols] = plane(p)[...]
    for copy in halo_copies:
        copy.wait_recv()
    for p in range(planes):
        from_next, from_prev = row_recv[0, p // 2], row_recv[1, p // 2]
        if p % 2 == 0:
            tile = jnp.where(low_sub, from_next, roll(from_prev, HALO, 0))
        else:
            tile = jnp.where(low_sub, roll(from_next, HALO, 0), from_prev)
        ext[p, rows:rext, 0:cols] = tile
    low8 = lax.broadcasted_iota(jnp.int32, (8, LANES), 0) < HALO
    from_right = jnp.concatenate(
        [col_recv[0], jnp.where(low8, corner_recv[0], corner_recv[2])], axis=0
    )
    from_left = jnp.concatenate(
        [col_recv[1], jnp.where(low8, corner_recv[1], corner_recv[3])], axis=0
    )
    near = lax.broadcasted_iota(jnp.int32, (rext, LANES), 1) < LANES // 2
    for p in range(planes):
        ext[p, :, cols:cext] = jnp.where(
            near, roll(from_right, -HALO * p, 1), roll(from_left, -HALO - HALO * p, 1)
        )

    ri = lax.broadcasted_iota(jnp.int32, (rext, cext), 0)
    ci = lax.broadcasted_iota(jnp.int32, (rext, cext), 1)
    r_lo = jnp.where(r < n_r - 1, rows + HALO, rows)
    r_hi = jnp.where(r > 0, rows + HALO, rext)
    c_lo = jnp.where(c < n_c - 1, cols + HALO, cols)
    c_hi = jnp.where(c > 0, cext - HALO, cext)
    inside = ((ri < r_lo) | (ri >= r_hi)) & ((ci < c_lo) | (ci >= c_hi))

    ext[mem] = jnp.where(inside, ext[mem], 0.0)
    ext[mem + 1] = jnp.where(inside, (0.5 * advect_rate) * ext[mem + 1], 0.0)
    ext[mem + 2] = jnp.where(inside, (0.5 * advect_rate) * ext[mem + 2], 0.0)

    def forward(m, carry):
        kap = jnp.where(inside, (0.5 * diffuse_rate) * jnp.exp(ext[m]), 0.0)
        v0, v1 = ext[mem + 1], ext[mem + 2]
        f_u, f_d = kap + roll(kap, -1, 0), kap + roll(kap, 1, 0)
        f_r, f_l = kap + roll(kap, -1, 1), kap + roll(kap, 1, 1)
        c_0 = jnp.where(inside, 1.0 - ((f_u + f_d) + (f_r + f_l)), 0.0)
        c_u = jnp.where(inside, f_u - v0, 0.0)
        c_d = jnp.where(inside, f_d + v0, 0.0)
        c_r = jnp.where(inside, f_r - v1, 0.0)
        c_l = jnp.where(inside, f_l + v1, 0.0)
        u = ext[mem]
        for _ in range(STEPS):
            u = (
                c_0 * u
                + (c_u * roll(u, -1, 0) + c_d * roll(u, 1, 0))
                + (c_r * roll(u, -1, 1) + c_l * roll(u, 1, 1))
            )
        field[pl.ds(pl.multiple_of(m * rows, rows), rows), :] = u[0:rows, 0:cols]
        return carry

    lax.fori_loop(0, mem, forward, 0)

    sens = sens_v[0]
    s_col = sens & (cols - 1)
    s_row = sens >> (cols.bit_length() - 1)
    n_s = sens.shape[1]
    hot_c = jnp.where(
        lax.broadcasted_iota(jnp.int32, (cols, n_s), 0) == s_col, 1.0, 0.0
    ).astype(jnp.bfloat16)
    f = field[...]
    f_hi, f_lo = split_bf16(f)
    f_lo2 = ((f - f_hi.astype(jnp.float32)) - f_lo.astype(jnp.float32)).astype(jnp.bfloat16)
    at_cols = dot32(f_hi, hot_c) + (dot32(f_lo, hot_c) + dot32(f_lo2, hot_c))
    hot_r = lax.broadcasted_iota(jnp.int32, (rows, n_s), 0) == s_row
    own = jnp.sum(
        jnp.where(hot_r[None], at_cols.reshape(mem, rows, n_s), 0.0), axis=1
    )
    mine = pl.ds(pl.multiple_of(e * mem, mem), mem)
    preds[mine, :] = own
    for m in range(mem):
        pred[m, 0] = own[m : m + 1]

    def spread(src, dst, ssem, rsem, ids):
        copies = []
        for d, device in enumerate(ids):
            copies.append(send(src, dst, ssem.at[d], rsem.at[d], device))
        return copies

    copies = spread(preds.at[mine], preds.at[mine], pred_ssem, pred_rsem, ens_ids)
    for copy in copies:
        copy.wait_recv()

    flat = preds[...]
    mean = jnp.sum(flat, axis=0, keepdims=True) * (1.0 / (n_e * mem))
    inv_noise = 1.0 / noise_v[0]
    weighted = (flat - mean) * inv_noise
    miss = (targ_v[0] - mean) * inv_noise
    members = n_e * mem
    against = jnp.concatenate(
        [weighted, miss, jnp.zeros((LANES - members - 1, n_s), jnp.float32)], axis=0
    )
    gram = lax.dot_general(
        preds[mine, :] - mean, against, (((1,), (1,)), ((), ())),
        precision=lax.Precision.HIGHEST, preferred_element_type=jnp.float32,
    )

    zbuf[z] = gram
    copies = spread(zbuf.at[z], zbuf.at[z], z_ssem, z_rsem, z_ids)

    def recv_half(slot, index, h):
        remote(part(index, h), part(index, h), th_ssem.at[slot], th_rsem.at[slot], to_o).wait_recv()

    near_l, near_r, far = x_l * 2 + core, x_r * 2 + core, x_f * 2 + core
    recv_half(0, near_l, 0)
    send_half(near_l, 0, 6, to_r)
    recv_half(3, near_r, 1)
    send_half(near_r, 1, 7, to_l)
    recv_half(1, near_l, 1)
    recv_half(2, near_r, 0)
    for h in range(2):
        send_half(near_l, h, 8 + h, to_o)
        send_half(near_r, h, 10 + h, to_o)

    for copy in copies:
        copy.wait_recv()
    ybuf[y] = jnp.sum(zbuf[...], axis=0)
    copies = spread(ybuf.at[y], ybuf.at[y], y_ssem, y_rsem, y_ids)
    for copy in copies:
        copy.wait_recv()
    gall[mine, :] = jnp.sum(ybuf[...], axis=0)
    copies = spread(gall.at[mine], gall.at[mine], g_ssem, g_rsem, ens_ids)

    recv_half(6, far, 0)
    send_half(far, 0, 12, to_o)
    recv_half(7, far, 1)
    send_half(far, 1, 13, to_o)

    for copy in copies:
        copy.wait_recv()

    arow = lax.broadcasted_iota(jnp.int32, (members, LANES), 0)
    acol = lax.broadcasted_iota(jnp.int32, (members, LANES), 1)
    first = members + 8
    unit = (arow == acol) | ((acol >= first) & (acol < first + mem) & (acol - first == arow - e * mem))
    aug = gall[...] * (1.0 / (members - 1)) + jnp.where(unit, 1.0, 0.0)
    for k in range(members):
        row_k = aug[k : k + 1, :]
        scaled = row_k / aug[k : k + 1, k : k + 1]
        col_k = aug[:, k : k + 1]
        aug = jnp.where(arow == k, scaled, aug - col_k * scaled)
    weight = aug[:, first : first + mem] + aug[:, members : members + 1]

    wide = members * 8
    pick = jnp.where(
        lax.broadcasted_iota(jnp.int32, (members, wide), 0)
        == lax.broadcasted_iota(jnp.int32, (members, wide), 1) // 8,
        1.0, 0.0,
    )
    spread_w = lax.dot_general(
        weight, pick, (((0,), (0,)), ((), ())),
        precision=lax.Precision.HIGHEST, preferred_element_type=jnp.float32,
    )
    big = jnp.broadcast_to(spread_w[:, None, :], (mem, 8, wide)).reshape(mem * 8, wide)
    same = (
        lax.broadcasted_iota(jnp.int32, (mem * 8, wide), 0) % 8
        == lax.broadcasted_iota(jnp.int32, (mem * 8, wide), 1) % 8
    )
    big = jnp.where(same, big, 0.0)
    b_hi, b_lo = split_bf16(big)

    recv_half(4, x * 2 + 1 - core, 0)
    recv_half(5, x * 2 + 1 - core, 1)
    for h in range(2):
        recv_half(8 + h, x_l * 2 + 1 - core, h)
        recv_half(10 + h, x_r * 2 + 1 - core, h)
        recv_half(12 + h, x_f * 2 + 1 - core, h)

    outs = []
    for t in range(rows // 8):
        tile = blocks[:, :, 8 * t : 8 * t + 8, :].reshape(wide, cols)
        t_hi, t_lo = split_bf16(tile)
        new = dot32(b_hi, t_hi) + (dot32(b_hi, t_lo) + dot32(b_lo, t_hi))
        result[:, 8 * t : 8 * t + 8, :] = new.reshape(mem, 8, cols)
        copy = pltpu.make_async_copy(
            result.at[:, pl.ds(8 * t, 8)], out.at[:, pl.ds(8 * t, 8)], out_sem.at[t]
        )
        copy.start()
        outs.append(copy)
    for copy in sends:
        copy.wait_send()
    for copy in outs:
        copy.wait()


def shards(sizes, theta, initial, velocity, sensors, target, noise):
    mem, rows, cols = theta.shape
    n_s = sensors.shape[-1]
    n_e, n_r, n_c, n_z = sizes
    n_y = n_r // n_z * n_c
    members = n_e * mem
    planes = mem + 3
    pairs = (planes + 1) // 2
    f32 = jnp.float32
    DMA = pltpu.SemaphoreType.DMA
    return pl.pallas_call(
        functools.partial(kernel, sizes),
        out_shape=(
            jax.ShapeDtypeStruct(theta.shape, f32),
            jax.ShapeDtypeStruct((mem, 1, 1, n_s), f32),
        ),
        in_specs=[pl.BlockSpec(memory_space=pl.ANY)] * 6,
        out_specs=(pl.BlockSpec(memory_space=pl.ANY), pl.BlockSpec(memory_space=pltpu.VMEM)),
        scratch_shapes=[
            pltpu.VMEM((n_e, mem, rows, cols), f32),
            pltpu.VMEM((3, rows, cols), f32),
            pltpu.VMEM((1, 1, n_s), jnp.int32),
            pltpu.VMEM((1, 1, n_s), f32),
            pltpu.VMEM((1, 1, n_s), f32),
            pltpu.VMEM((2, pairs, 8, cols), f32),
            pltpu.VMEM((2, pairs, 8, cols), f32),
            pltpu.VMEM((2, rows, LANES), f32),
            pltpu.VMEM((2, rows, LANES), f32),
            pltpu.VMEM((4, 8, LANES), f32),
            pltpu.VMEM((planes, rows + 2 * HALO, cols + LANES), f32),
            pltpu.VMEM((mem * rows, cols), f32),
            pltpu.VMEM((members, n_s), f32),
            pltpu.VMEM((n_z, mem, LANES), f32),
            pltpu.VMEM((n_y, mem, LANES), f32),
            pltpu.VMEM((members, LANES), f32),
            pltpu.VMEM((mem, rows, cols), f32),
            DMA((6,)),
            DMA((8,)), DMA((8,)),
            DMA((n_e - 1,)), DMA((n_e - 1,)),
            DMA((n_z - 1,)), DMA((n_z - 1,)),
            DMA((n_y - 1,)), DMA((n_y - 1,)),
            DMA((n_e - 1,)), DMA((n_e - 1,)),
            DMA((14,)), DMA((14,)),
            DMA((rows // 8,)),
        ],
        compiler_params=pltpu.CompilerParams(
            collective_id=0, has_side_effects=True, vmem_limit_bytes=48 * 1024 * 1024
        ),
    )(theta, initial, velocity, sensors, target, noise)


def solution(mesh):
    in_specs = (
        P("ens", "row", "col"),
        P("row", "col"),
        P(None, "row", "col"),
        P("row", "col", None),
        P("row", "col", None),
        P("row", "col", None),
    )
    out_specs = (P("ens", "row", "col"), P("ens", "row", "col", None))
    n_r = mesh.shape["row"]
    sizes = (mesh.shape["ens"], n_r, mesh.shape["col"], n_r // 2)
    return jax.shard_map(
        functools.partial(shards, sizes),
        mesh=mesh, in_specs=in_specs, out_specs=out_specs, check_vma=False,
    )
```

```python
import functools

import jax
import jax.numpy as jnp
from jax import lax
from jax.experimental import pallas as pl
from jax.experimental.pallas import tpu as pltpu
from jax.sharding import PartitionSpec as P

STEPS = 4
diffuse_rate = 0.07
advect_rate = 0.3

MESH = pl.DeviceIdType.MESH
HALO = 4
LANES = 128


def roll(x, shift, axis):
    shift = shift % x.shape[axis]
    return x if shift == 0 else pltpu.roll(x, shift, axis)


def split_bf16(x):
    hi = x.astype(jnp.bfloat16)
    lo = (x - hi.astype(jnp.float32)).astype(jnp.bfloat16)
    return hi, lo


def dot32(a, b):
    return jnp.dot(a, b, preferred_element_type=jnp.float32)


def eliminate(aug, n, p):
    arow = lax.broadcasted_iota(jnp.int32, aug.shape, 0)
    for k in range(0, n, p):
        col = [jnp.broadcast_to(aug[:, k + j : k + j + 1], aug.shape) for j in range(p)]
        d = [[col[j][k + i : k + i + 1, :] for j in range(p)] for i in range(p)]
        new = [aug[k + i : k + i + 1, :] for i in range(p)]
        for i in range(p):
            inv = 1.0 / d[i][i]
            for j in range(i + 1, p):
                d[i][j] = d[i][j] * inv
            new[i] = new[i] * inv
            for q in range(p):
                if q != i:
                    for j in range(i + 1, p):
                        d[q][j] = d[q][j] - d[q][i] * d[i][j]
                    new[q] = new[q] - d[q][i] * new[i]
        less = col[0] * new[0]
        for j in range(1, p):
            less = less + col[j] * new[j]
        aug = aug - less
        for j in range(p):
            aug = jnp.where(arow == k + j, new[j], aug)
    return aug


def kernel(
    sizes,
    theta, initial, velocity, sensors, target, noise,
    out, pred,
    blocks, logk, extra, frame, sens_v, targ_v, noise_v,
    col_send, col_recv, corner_recv,
    kap, c_0, c_u, c_d, c_r, c_l, u_0, u_1, u_2, u_3, field,
    preds, zbuf, ybuf, gall, result,
    load_sem, halo_ssem, halo_rsem, pred_ssem, pred_rsem,
    z_ssem, z_rsem, y_ssem, y_rsem, g_ssem, g_rsem,
    th_ssem, th_rsem, out_sem,
):
    n_e, n_r, n_c, n_z = sizes
    n_x = n_e // 2
    n_yh = n_r // n_z
    n_y = n_yh * n_c
    mem, rows, cols = theta.shape
    cext = cols + LANES
    e, r, c = lax.axis_index("ens"), lax.axis_index("row"), lax.axis_index("col")
    x, core = e // 2, e % 2
    yh, z = r // n_z, r % n_z
    y = yh * n_c + c

    loads = [
        pltpu.make_async_copy(theta, blocks.at[e], load_sem.at[0]),
        pltpu.make_async_copy(initial, extra.at[0, pl.ds(8, rows)], load_sem.at[1]),
        pltpu.make_async_copy(
            velocity, extra.at[pl.ds(1, 2), pl.ds(8, rows)], load_sem.at[2]
        ),
        pltpu.make_async_copy(sensors, sens_v, load_sem.at[3]),
        pltpu.make_async_copy(target, targ_v, load_sem.at[4]),
        pltpu.make_async_copy(noise, noise_v, load_sem.at[5]),
    ]
    for copy in loads:
        copy.start()

    prev, nxt = (r + n_r - 1) % n_r, (r + 1) % n_r
    left, right = (c + n_c - 1) % n_c, (c + 1) % n_c
    halo_ids = [
        {"row": prev}, {"row": nxt}, {"col": left}, {"col": right},
        {"row": prev, "col": left}, {"row": prev, "col": right},
        {"row": nxt, "col": left}, {"row": nxt, "col": right},
    ]
    ens_ids = [{"ens": (e + d) % n_e} for d in range(1, n_e)]
    z_ids = [{"row": yh * n_z + (z + d) % n_z} for d in range(1, n_z)]
    y_ids = []
    for dy in sorted(range(n_y), key=lambda d: -min(d, n_y - d)):
        for dx in sorted(range(n_x), key=lambda d: -min(d, n_x - d)):
            if dx or dy:
                other = (y + dy) % n_y
                y_ids.append({
                    "ens": (x + dx) % n_x * 2 + core,
                    "row": other // n_c * n_z + z,
                    "col": other % n_c,
                })

    barrier = pltpu.get_barrier_semaphore()
    everyone = halo_ids + ens_ids + z_ids + y_ids
    for device in everyone:
        pl.semaphore_signal(barrier, inc=1, device_id=device, device_id_type=MESH)
    pl.semaphore_wait(barrier, len(everyone))

    sends = []

    def remote(src, dst, ssem, rsem, device):
        copy = pltpu.make_async_remote_copy(
            src_ref=src, dst_ref=dst, send_sem=ssem, recv_sem=rsem,
            device_id=device, device_id_type=MESH,
        )
        return copy

    def send(*args):
        copy = remote(*args)
        copy.start()
        sends.append(copy)
        return copy

    for copy in loads:
        copy.wait()

    half = mem // 2
    x_r, x_l, x_f = (x + 1) % n_x, (x + n_x - 1) % n_x, (x + 2) % n_x
    to_r, to_l = {"ens": x_r * 2 + core}, {"ens": x_l * 2 + core}
    to_o = {"ens": x * 2 + (1 - core)}

    def part(index, h):
        return blocks.at[index, pl.ds(h * half, half)]

    def send_half(index, h, slot, device):
        return send(part(index, h), part(index, h), th_ssem.at[slot], th_rsem.at[slot], device)

    def turned(t):
        tile = blocks[e, :, 8 * t : 8 * t + 8, :]
        logk[HALO + 8 * t : HALO + 8 * t + 8] = jnp.swapaxes(tile, 0, 1)

    last = rows // 8 - 1
    turned(0)
    turned(last)

    def send_halo(k, src, dst, device):
        send(src, dst, halo_ssem.at[k], halo_rsem.at[k], device)

    def edge(start):
        return logk.at[pl.ds(start, HALO)]

    def edge_x(start):
        return extra.at[:, pl.ds(start, 8)]

    send_halo(0, edge(HALO), edge(rows + HALO), halo_ids[0])
    send_halo(1, edge(rows), edge(0), halo_ids[1])
    send_halo(2, edge_x(8), edge_x(rows + 8), halo_ids[0])
    send_halo(3, edge_x(rows), edge_x(0), halo_ids[1])
    for t in range(1, last):
        turned(t)

    lane = lax.broadcasted_iota(jnp.int32, (8, LANES), 1)
    slot_of = lane // HALO
    per = LANES // HALO
    for side in range(2):
        low = 0 if side == 0 else cols - LANES
        off = 0 if side == 0 else HALO
        for half_t, first_row in ((0, 0), (2, per)):
            acc = jnp.zeros((8, LANES), jnp.float32)
            for k in range(per):
                row = logk[HALO + first_row + k, :, low : low + LANES]
                acc = jnp.where(slot_of == k, roll(row, HALO * k + off, 1), acc)
            col_send[side, half_t] = acc
        acc = jnp.zeros((8, LANES), jnp.float32)
        for p in range(3):
            for t in range(last + 1):
                k = p * (last + 1) + t
                row = extra[p, 8 + 8 * t : 16 + 8 * t, low : low + LANES]
                acc = jnp.where(slot_of == k, roll(row, HALO * k + off, 1), acc)
        col_send[side, 1] = acc
        send_halo(4 + side, col_send.at[side], col_recv.at[side], halo_ids[2 + side])
    for k in range(4):
        part_k = pl.ds(0 if k < 2 else 1, 2)
        send_halo(6 + k, col_send.at[k % 2, part_k], corner_recv.at[k], halo_ids[4 + k])
    halo_copies = list(sends)

    for h in range(2):
        send_half(e, h, h, to_r)
        send_half(e, 1 - h, 2 + 1 - h, to_l)
    for h in range(2):
        send_half(e, h, 4 + h, to_o)

    ci = lax.broadcasted_iota(jnp.int32, (8, cext), 1)
    c_lo = jnp.where(c < n_c - 1, cols + HALO, cols)
    c_hi = jnp.where(c > 0, cext - HALO, cext)
    ok_mid = (ci < c_lo) | (ci >= c_hi)
    ok_top = ok_mid & (r > 0)
    ok_bot = ok_mid & (r < n_r - 1)
    near = lane < LANES // 2
    half_d, half_a = 0.5 * diffuse_rate, 0.5 * advect_rate

    def unpack(from_right, from_left, k):
        return jnp.where(near, roll(from_right, -HALO * k, 1), roll(from_left, -HALO - HALO * k, 1))

    def fill_kap(i, ok, from_right, from_left, k):
        kap[i, :, 0:cols] = jnp.where(ok[:, 0:cols], half_d * jnp.exp(logk[i]), 0.0)
        outer = unpack(from_right, from_left, k)
        kap[i, :, cols:cext] = jnp.where(ok[:, cols:cext], half_d * jnp.exp(outer), 0.0)

    def fill_extra(t, ok, from_right, from_left, slot_t):
        at = slice(8 * t, 8 * t + 8)
        for p in range(3):
            scale = 1.0 if p == 0 else half_a
            outer = unpack(from_right, from_left, p * (last + 1) + slot_t)
            frame[p, at, 0:cols] = jnp.where(ok[:, 0:cols], scale * extra[p, at], 0.0)
            frame[p, at, cols:cext] = jnp.where(ok[:, cols:cext], scale * outer, 0.0)

    def coefficients(i, ok, v0, v1):
        k = kap[i]
        f_u, f_d = k + kap[i + 1], k + kap[i - 1]
        f_r, f_l = k + roll(k, -1, 1), k + roll(k, 1, 1)
        c_0[i] = jnp.where(ok, 1.0 - ((f_u + f_d) + (f_r + f_l)), 0.0)
        c_u[i] = jnp.where(ok, f_u - v0, 0.0)
        c_d[i] = jnp.where(ok, f_d + v0, 0.0)
        c_r[i] = jnp.where(ok, f_r - v1, 0.0)
        c_l[i] = jnp.where(ok, f_l + v1, 0.0)

    def step(src, i):
        u = src[i]
        return (
            c_0[i] * u
            + (c_u[i] * src[i + 1] + c_d[i] * src[i - 1])
            + (c_r[i] * roll(u, -1, 1) + c_l[i] * roll(u, 1, 1))
        )

    states = [u_0, u_1, u_2, u_3]

    for copy in halo_copies[4:6]:
        copy.wait_recv()
    for t in range(last + 1):
        fill_extra(t + 1, ok_mid, col_recv[0, 1], col_recv[1, 1], t)
    for i in range(rows):
        tile = 0 if i < per else 2
        fill_kap(HALO + i, ok_mid, col_recv[0, tile], col_recv[1, tile], i % per)

    def first(t, carry):
        at = pl.ds(pl.multiple_of(8 * t + 8, 8), 8)
        u, v0, v1 = frame[0, at, :], frame[1, at, :], frame[2, at, :]
        for j in range(8):
            i = HALO + 8 * t + j
            u_0[i] = jnp.broadcast_to(u[j : j + 1], (8, cext))
            coefficients(i, ok_mid, v0[j : j + 1], v1[j : j + 1])
        return carry

    lax.fori_loop(0, last + 1, first, 0)
    for s in range(STEPS):
        def chunk(t, carry, s=s):
            for j in range(8):
                i = HALO + 8 * t + j
                new = step(states[s], i)
                if s < STEPS - 1:
                    states[s + 1][i] = new
                else:
                    field[pl.ds(pl.multiple_of(64 * t + 8 * j, 8), 8), :] = new[:, 0:cols]
            return carry
        lax.fori_loop(0, last + 1, chunk, 0)

    sens = sens_v[0]
    n_s = sens.shape[1]
    s_col = sens & (cols - 1)
    s_row = jnp.broadcast_to(sens >> (cols.bit_length() - 1), (8, n_s))
    hot_c = jnp.where(
        lax.broadcasted_iota(jnp.int32, (cols, n_s), 0) == s_col, 1.0, 0.0
    ).astype(jnp.bfloat16)

    def sensed(first_row, count, acc):
        f = field[8 * first_row : 8 * (first_row + count), :]
        f_hi, f_lo = split_bf16(f)
        f_lo2 = ((f - f_hi.astype(jnp.float32)) - f_lo.astype(jnp.float32)).astype(jnp.bfloat16)
        at = dot32(f_hi, hot_c) + (dot32(f_lo, hot_c) + dot32(f_lo2, hot_c))
        for j in range(count):
            acc = jnp.where(s_row == first_row + j, at[8 * j : 8 * j + 8], acc)
        return acc

    own = sensed(8, rows - 16, jnp.zeros((mem, n_s), jnp.float32))

    for copy in halo_copies[0:4] + halo_copies[6:10]:
        copy.wait_recv()
    fill_extra(0, ok_top, corner_recv[2, 0], corner_recv[3, 0], last)
    fill_extra(last + 2, ok_bot, corner_recv[0, 1], corner_recv[1, 1], 0)
    for k in range(HALO):
        fill_kap(k, ok_top, corner_recv[2, 1], corner_recv[3, 1], per - HALO + k)
        fill_kap(HALO + rows + k, ok_bot, corner_recv[0, 0], corner_recv[1, 0], k)

    def row_of(p, i):
        return frame[p, i + 4 : i + 5, :]

    for k in range(HALO):
        u_0[k] = jnp.broadcast_to(row_of(0, k), (8, cext))
        i = HALO + rows + k
        u_0[i] = jnp.broadcast_to(row_of(0, i), (8, cext))
    for i in range(1, HALO + 1):
        j = 2 * HALO + rows - 1 - i
        coefficients(i, ok_top if i < HALO else ok_mid, row_of(1, i), row_of(2, i))
        coefficients(j, ok_bot if i < HALO else ok_mid, row_of(1, j), row_of(2, j))
    for s in range(STEPS):
        for i in range(1 + s, HALO + 1 + s):
            j = 2 * HALO + rows - 1 - i
            for q in (i, j):
                new = step(states[s], q)
                if s < STEPS - 1:
                    states[s + 1][q] = new
                else:
                    field[8 * (q - HALO) : 8 * (q - HALO) + 8, :] = new[:, 0:cols]
    own = sensed(0, 8, own)
    own = sensed(rows - 8, 8, own)
    mine = pl.ds(pl.multiple_of(e * mem, mem), mem)
    preds[mine, :] = own
    for m in range(mem):
        pred[m, 0] = own[m : m + 1]

    def spread(src, dst, ssem, rsem, ids):
        copies = []
        for d, device in enumerate(ids):
            copies.append(send(src, dst, ssem.at[d], rsem.at[d], device))
        return copies

    copies = spread(preds.at[mine], preds.at[mine], pred_ssem, pred_rsem, ens_ids)
    for copy in copies:
        copy.wait_recv()

    flat = preds[...]
    mean = jnp.sum(flat, axis=0, keepdims=True) * (1.0 / (n_e * mem))
    inv_noise = 1.0 / noise_v[0]
    weighted = (flat - mean) * inv_noise
    miss = (targ_v[0] - mean) * inv_noise
    members = n_e * mem
    against = jnp.concatenate(
        [weighted, miss, jnp.zeros((LANES - members - 1, n_s), jnp.float32)], axis=0
    )
    gram = lax.dot_general(
        preds[mine, :] - mean, against, (((1,), (1,)), ((), ())),
        precision=lax.Precision.HIGHEST, preferred_element_type=jnp.float32,
    )

    zbuf[z] = gram
    copies = spread(zbuf.at[z], zbuf.at[z], z_ssem, z_rsem, z_ids)

    def recv_half(slot, index, h):
        remote(part(index, h), part(index, h), th_ssem.at[slot], th_rsem.at[slot], to_o).wait_recv()

    near_l, near_r, far = x_l * 2 + core, x_r * 2 + core, x_f * 2 + core
    recv_half(0, near_l, 0)
    send_half(near_l, 0, 6, to_r)
    recv_half(3, near_r, 1)
    send_half(near_r, 1, 7, to_l)
    recv_half(1, near_l, 1)
    recv_half(2, near_r, 0)
    for h in range(2):
        send_half(near_l, h, 8 + h, to_o)
        send_half(near_r, h, 10 + h, to_o)

    for copy in copies:
        copy.wait_recv()
    ybuf[x, y] = jnp.sum(zbuf[...], axis=0)
    copies = spread(ybuf.at[x, y], ybuf.at[x, y], y_ssem, y_rsem, y_ids)
    for copy in copies:
        copy.wait_recv()
    gall[core] = jnp.sum(ybuf[...], axis=1)
    copies = [send(gall.at[core], gall.at[core], g_ssem.at[0], g_rsem.at[0], to_o)]

    recv_half(6, far, 0)
    send_half(far, 0, 12, to_o)
    recv_half(7, far, 1)
    send_half(far, 1, 13, to_o)

    for copy in copies:
        copy.wait_recv()

    arow = lax.broadcasted_iota(jnp.int32, (members, LANES), 0)
    acol = lax.broadcasted_iota(jnp.int32, (members, LANES), 1)
    first = members + 8
    unit = (arow == acol) | ((acol >= first) & (acol < first + mem) & (acol - first == arow - e * mem))
    sums = jnp.concatenate([gall[i % 2, i // 2] for i in range(n_e)], axis=0)
    aug = sums * (1.0 / (members - 1)) + jnp.where(unit, 1.0, 0.0)
    aug = eliminate(aug, members, 8)
    weight = aug[:, first : first + mem] + aug[:, members : members + 1]

    wide = members * 8
    pick = jnp.where(
        lax.broadcasted_iota(jnp.int32, (members, wide), 0)
        == lax.broadcasted_iota(jnp.int32, (members, wide), 1) // 8,
        1.0, 0.0,
    )
    spread_w = lax.dot_general(
        weight, pick, (((0,), (0,)), ((), ())),
        precision=lax.Precision.HIGHEST, preferred_element_type=jnp.float32,
    )
    big = jnp.broadcast_to(spread_w[:, None, :], (mem, 8, wide)).reshape(mem * 8, wide)
    same = (
        lax.broadcasted_iota(jnp.int32, (mem * 8, wide), 0) % 8
        == lax.broadcasted_iota(jnp.int32, (mem * 8, wide), 1) % 8
    )
    big = jnp.where(same, big, 0.0)
    b_hi, b_lo = split_bf16(big)
    b_both = jnp.concatenate([b_hi, b_lo], axis=0)

    recv_half(4, x * 2 + 1 - core, 0)
    recv_half(5, x * 2 + 1 - core, 1)
    for h in range(2):
        recv_half(8 + h, x_l * 2 + 1 - core, h)
        recv_half(10 + h, x_r * 2 + 1 - core, h)
        recv_half(12 + h, x_f * 2 + 1 - core, h)

    outs = []
    for t in range(rows // 8):
        tile = blocks[:, :, 8 * t : 8 * t + 8, :].reshape(wide, cols)
        t_hi, t_lo = split_bf16(tile)
        two = dot32(b_both, t_hi)
        new = two[: mem * 8] + (dot32(b_hi, t_lo) + two[mem * 8 :])
        result[:, 8 * t : 8 * t + 8, :] = new.reshape(mem, 8, cols)
        copy = pltpu.make_async_copy(
            result.at[:, pl.ds(8 * t, 8)], out.at[:, pl.ds(8 * t, 8)], out_sem.at[t]
        )
        copy.start()
        outs.append(copy)
    for copy in sends:
        copy.wait_send()
    for copy in outs:
        copy.wait()


def shards(sizes, theta, initial, velocity, sensors, target, noise):
    mem, rows, cols = theta.shape
    n_s = sensors.shape[-1]
    n_e, n_r, n_c, n_z = sizes
    n_y = n_r // n_z * n_c
    members = n_e * mem
    rext, cext = rows + 2 * HALO, cols + LANES
    f32 = jnp.float32
    DMA = pltpu.SemaphoreType.DMA
    return pl.pallas_call(
        functools.partial(kernel, sizes),
        out_shape=(
            jax.ShapeDtypeStruct(theta.shape, f32),
            jax.ShapeDtypeStruct((mem, 1, 1, n_s), f32),
        ),
        in_specs=[pl.BlockSpec(memory_space=pltpu.HBM)] * 6,
        out_specs=(pl.BlockSpec(memory_space=pltpu.HBM), pl.BlockSpec(memory_space=pltpu.VMEM)),
        scratch_shapes=[
            pltpu.VMEM((n_e, mem, rows, cols), f32),
            pltpu.VMEM((rext, mem, cols), f32),
            pltpu.VMEM((3, rows + 16, cols), f32),
            pltpu.VMEM((3, rows + 16, cext), f32),
            pltpu.VMEM((1, 1, n_s), jnp.int32),
            pltpu.VMEM((1, 1, n_s), f32),
            pltpu.VMEM((1, 1, n_s), f32),
            pltpu.VMEM((2, 3, 8, LANES), f32),
            pltpu.VMEM((2, 3, 8, LANES), f32),
            pltpu.VMEM((4, 2, 8, LANES), f32),
            *[pltpu.VMEM((rext, mem, cext), f32)] * 10,
            pltpu.VMEM((mem * rows, cols), f32),
            pltpu.VMEM((members, n_s), f32),
            pltpu.VMEM((n_z, mem, LANES), f32),
            pltpu.VMEM((n_e // 2, n_y, mem, LANES), f32),
            pltpu.VMEM((2, n_e // 2, mem, LANES), f32),
            pltpu.VMEM((mem, rows, cols), f32),
            DMA((6,)),
            DMA((10,)), DMA((10,)),
            DMA((n_e - 1,)), DMA((n_e - 1,)),
            DMA((n_z - 1,)), DMA((n_z - 1,)),
            DMA((n_e // 2 * n_y - 1,)), DMA((n_e // 2 * n_y - 1,)),
            DMA((1,)), DMA((1,)),
            DMA((14,)), DMA((14,)),
            DMA((rows // 8,)),
        ],
        compiler_params=pltpu.CompilerParams(
            collective_id=0, has_side_effects=True, vmem_limit_bytes=48 * 1024 * 1024
        ),
    )(*(pltpu.with_memory_space_constraint(a, pltpu.HBM)
        for a in (theta, initial, velocity, sensors, target, noise)))


def solution(mesh):
    in_specs = (
        P("ens", "row", "col"),
        P("row", "col"),
        P(None, "row", "col"),
        P("row", "col", None),
        P("row", "col", None),
        P("row", "col", None),
    )
    out_specs = (P("ens", "row", "col"), P("ens", "row", "col", None))
    n_r = mesh.shape["row"]
    sizes = (mesh.shape["ens"], n_r, mesh.shape["col"], n_r // 2)
    return jax.shard_map(
        functools.partial(shards, sizes),
        mesh=mesh, in_specs=in_specs, out_specs=out_specs, check_vma=False,
    )
```

```python
import functools

import jax
import jax.numpy as jnp
from jax import lax
from jax.experimental import pallas as pl
from jax.experimental.pallas import tpu as pltpu
from jax.sharding import PartitionSpec as P

STEPS = 4
diffuse_rate = 0.07
advect_rate = 0.3

MESH = pl.DeviceIdType.MESH
HALO = 4
LANES = 128


def roll(x, shift, axis):
    shift = shift % x.shape[axis]
    return x if shift == 0 else pltpu.roll(x, shift, axis)


def split_bf16(x):
    hi = x.astype(jnp.bfloat16)
    lo = (x - hi.astype(jnp.float32)).astype(jnp.bfloat16)
    return hi, lo


def dot32(a, b):
    return jnp.dot(a, b, preferred_element_type=jnp.float32)


def eliminate(aug, n, p):
    arow = lax.broadcasted_iota(jnp.int32, aug.shape, 0)
    for k in range(0, n, p):
        col = [jnp.broadcast_to(aug[:, k + j : k + j + 1], aug.shape) for j in range(p)]
        d = [[col[j][k + i : k + i + 1, :] for j in range(p)] for i in range(p)]
        new = [aug[k + i : k + i + 1, :] for i in range(p)]
        for i in range(p):
            inv = 1.0 / d[i][i]
            for j in range(i + 1, p):
                d[i][j] = d[i][j] * inv
            new[i] = new[i] * inv
            for q in range(p):
                if q != i:
                    for j in range(i + 1, p):
                        d[q][j] = d[q][j] - d[q][i] * d[i][j]
                    new[q] = new[q] - d[q][i] * new[i]
        less = col[0] * new[0]
        for j in range(1, p):
            less = less + col[j] * new[j]
        aug = aug - less
        for j in range(p):
            aug = jnp.where(arow == k + j, new[j], aug)
    return aug


def kernel(
    sizes,
    theta, initial, velocity, sensors, target, noise,
    out, pred,
    blocks, logk, extra, frame, sens_v, targ_v, noise_v,
    col_send, col_recv, corner_recv,
    kap, c_0, c_u, c_d, c_r, c_l, u_0, u_1, u_2, u_3, field,
    preds, zbuf, ybuf, gall, th_hi, th_lo, result,
    load_sem, halo_ssem, halo_rsem, pred_ssem, pred_rsem,
    z_ssem, z_rsem, y_ssem, y_rsem, g_ssem, g_rsem,
    th_ssem, th_rsem, out_sem, relay_sem,
):
    n_e, n_r, n_c, n_z = sizes
    n_x = n_e // 2
    n_yh = n_r // n_z
    n_y = n_yh * n_c
    mem, rows, cols = theta.shape
    cext = cols + LANES
    e, r, c = lax.axis_index("ens"), lax.axis_index("row"), lax.axis_index("col")
    x, core = e // 2, e % 2
    yh, z = r // n_z, r % n_z
    y = yh * n_c + c

    loads = [
        pltpu.make_async_copy(theta, blocks.at[e], load_sem.at[0]),
        pltpu.make_async_copy(initial, extra.at[0, pl.ds(8, rows)], load_sem.at[1]),
        pltpu.make_async_copy(
            velocity, extra.at[pl.ds(1, 2), pl.ds(8, rows)], load_sem.at[2]
        ),
        pltpu.make_async_copy(sensors, sens_v, load_sem.at[3]),
        pltpu.make_async_copy(target, targ_v, load_sem.at[4]),
        pltpu.make_async_copy(noise, noise_v, load_sem.at[5]),
    ]
    for copy in loads:
        copy.start()

    prev, nxt = (r + n_r - 1) % n_r, (r + 1) % n_r
    left, right = (c + n_c - 1) % n_c, (c + 1) % n_c
    halo_ids = [
        {"row": prev}, {"row": nxt}, {"col": left}, {"col": right},
        {"row": prev, "col": left}, {"row": prev, "col": right},
        {"row": nxt, "col": left}, {"row": nxt, "col": right},
    ]
    ens_ids = [{"ens": (e + d) % n_e} for d in range(1, n_e)]
    z_ids = [{"row": yh * n_z + (z + d) % n_z} for d in range(1, n_z)]
    y_ids = []
    for dy in sorted(range(n_y), key=lambda d: -min(d, n_y - d)):
        for dx in sorted(range(n_x), key=lambda d: -min(d, n_x - d)):
            if dx or dy:
                other = (y + dy) % n_y
                y_ids.append({
                    "ens": (x + dx) % n_x * 2 + core,
                    "row": other // n_c * n_z + z,
                    "col": other % n_c,
                })

    has_p, has_n, has_l, has_r = r > 0, r < n_r - 1, c > 0, c < n_c - 1
    halo_out = [
        has_p, has_n, has_l, has_r, has_p & has_l, has_p & has_r, has_n & has_l, has_n & has_r
    ]
    halo_in = [
        has_n, has_p, has_r, has_l, has_n & has_r, has_n & has_l, has_p & has_r, has_p & has_l
    ]
    x_r, x_l, x_f = (x + 1) % n_x, (x + n_x - 1) % n_x, (x + 2) % n_x
    to_r, to_l = {"ens": x_r * 2 + core}, {"ens": x_l * 2 + core}
    to_o = {"ens": x * 2 + (1 - core)}
    y_r, y_l = (y + 1) % n_y, (y + n_y - 1) % n_y
    near_ids = [
        to_r, to_l, to_o,
        {"row": yh * n_z + (z + 1) % n_z}, {"row": yh * n_z + (z + n_z - 1) % n_z},
        {"row": y_r // n_c * n_z + z, "col": y_r % n_c},
        {"row": y_l // n_c * n_z + z, "col": y_l % n_c},
    ]

    barrier = pltpu.get_barrier_semaphore()
    for device in near_ids:
        pl.semaphore_signal(barrier, inc=1, device_id=device, device_id_type=MESH)
    for device, there in zip(halo_ids, halo_out, strict=True):
        @pl.when(there)
        def _(device=device):
            pl.semaphore_signal(barrier, inc=1, device_id=device, device_id_type=MESH)
    one = [jnp.where(v, 1, 0) for v in (has_p, has_n, has_l, has_r)]
    n_halo = (1 + one[0] + one[1]) * (1 + one[2] + one[3]) - 1
    pl.semaphore_wait(barrier, len(near_ids) + n_halo)

    def relay_signal(j):
        for device in near_ids:
            pl.semaphore_signal(
                relay_sem.at[j], inc=1, device_id=device, device_id_type=MESH
            )

    def relay_wait(j):
        pl.semaphore_wait(relay_sem.at[j], len(near_ids))
        if j < 2:
            relay_signal(j + 1)

    relay_signal(0)
    sends = []

    def remote(src, dst, ssem, rsem, device):
        copy = pltpu.make_async_remote_copy(
            src_ref=src, dst_ref=dst, send_sem=ssem, recv_sem=rsem,
            device_id=device, device_id_type=MESH,
        )
        return copy

    def send(*args):
        copy = remote(*args)
        copy.start()
        sends.append(copy)
        return copy

    for copy in loads:
        copy.wait()

    half = mem // 2

    def part(index, h):
        return blocks.at[index, pl.ds(h * half, half)]

    def send_half(index, h, slot, device):
        return send(part(index, h), part(index, h), th_ssem.at[slot], th_rsem.at[slot], device)

    def turned(t):
        tile = blocks[e, :, 8 * t : 8 * t + 8, :]
        logk[HALO + 8 * t : HALO + 8 * t + 8] = jnp.swapaxes(tile, 0, 1)

    last = rows // 8 - 1
    turned(0)
    turned(last)

    halo_copies = []

    def send_halo(k, src, dst, which):
        copy = remote(src, dst, halo_ssem.at[k], halo_rsem.at[k], halo_ids[which])
        pl.when(halo_out[which])(copy.start)
        halo_copies.append((copy, halo_out[which], halo_in[which]))

    def wait_halo(k):
        copy, _, there = halo_copies[k]
        pl.when(there)(copy.wait_recv)

    def edge(start):
        return logk.at[pl.ds(start, HALO)]

    def edge_x(start):
        return extra.at[:, pl.ds(start, 8)]

    send_halo(0, edge(HALO), edge(rows + HALO), 0)
    send_halo(1, edge(rows), edge(0), 1)
    send_halo(2, edge_x(8), edge_x(rows + 8), 0)
    send_halo(3, edge_x(rows), edge_x(0), 1)
    for t in range(1, last):
        turned(t)

    lane = lax.broadcasted_iota(jnp.int32, (8, LANES), 1)
    slot_of = lane // HALO
    per = LANES // HALO
    for side in range(2):
        low = 0 if side == 0 else cols - LANES
        off = 0 if side == 0 else HALO
        for half_t, first_row in ((0, 0), (2, per)):
            acc = jnp.zeros((8, LANES), jnp.float32)
            for k in range(per):
                row = logk[HALO + first_row + k, :, low : low + LANES]
                acc = jnp.where(slot_of == k, roll(row, HALO * k + off, 1), acc)
            col_send[side, half_t] = acc
        acc = jnp.zeros((8, LANES), jnp.float32)
        for p in range(3):
            for t in range(last + 1):
                k = p * (last + 1) + t
                row = extra[p, 8 + 8 * t : 16 + 8 * t, low : low + LANES]
                acc = jnp.where(slot_of == k, roll(row, HALO * k + off, 1), acc)
        col_send[side, 1] = acc
        send_halo(4 + side, col_send.at[side], col_recv.at[side], 2 + side)
    for k in range(4):
        part_k = pl.ds(0 if k < 2 else 1, 2)
        send_halo(6 + k, col_send.at[k % 2, part_k], corner_recv.at[k], 4 + k)

    for h in range(2):
        send_half(e, h, h, to_r)
        send_half(e, 1 - h, 2 + 1 - h, to_l)
    for h in range(2):
        send_half(e, h, 4 + h, to_o)

    ci = lax.broadcasted_iota(jnp.int32, (8, cext), 1)
    c_lo = jnp.where(c < n_c - 1, cols + HALO, cols)
    c_hi = jnp.where(c > 0, cext - HALO, cext)
    ok_mid = (ci < c_lo) | (ci >= c_hi)
    ok_top = ok_mid & (r > 0)
    ok_bot = ok_mid & (r < n_r - 1)
    near = lane < LANES // 2
    half_d, half_a = 0.5 * diffuse_rate, 0.5 * advect_rate

    def unpack(from_right, from_left, k):
        return jnp.where(near, roll(from_right, -HALO * k, 1), roll(from_left, -HALO - HALO * k, 1))

    def fill_kap(i, ok, from_right, from_left, k):
        kap[i, :, 0:cols] = jnp.where(ok[:, 0:cols], half_d * jnp.exp(logk[i]), 0.0)
        outer = unpack(from_right, from_left, k)
        kap[i, :, cols:cext] = jnp.where(ok[:, cols:cext], half_d * jnp.exp(outer), 0.0)

    def fill_extra(t, ok, from_right, from_left, slot_t):
        at = slice(8 * t, 8 * t + 8)
        for p in range(3):
            scale = 1.0 if p == 0 else half_a
            outer = unpack(from_right, from_left, p * (last + 1) + slot_t)
            frame[p, at, 0:cols] = jnp.where(ok[:, 0:cols], scale * extra[p, at], 0.0)
            frame[p, at, cols:cext] = jnp.where(ok[:, cols:cext], scale * outer, 0.0)

    def coefficients(i, ok, v0, v1):
        k = kap[i]
        f_u, f_d = k + kap[i + 1], k + kap[i - 1]
        f_r, f_l = k + roll(k, -1, 1), k + roll(k, 1, 1)
        c_0[i] = jnp.where(ok, 1.0 - ((f_u + f_d) + (f_r + f_l)), 0.0)
        c_u[i] = jnp.where(ok, f_u - v0, 0.0)
        c_d[i] = jnp.where(ok, f_d + v0, 0.0)
        c_r[i] = jnp.where(ok, f_r - v1, 0.0)
        c_l[i] = jnp.where(ok, f_l + v1, 0.0)

    def step(src, i):
        u = src[i]
        return (
            c_0[i] * u
            + (c_u[i] * src[i + 1] + c_d[i] * src[i - 1])
            + (c_r[i] * roll(u, -1, 1) + c_l[i] * roll(u, 1, 1))
        )

    states = [u_0, u_1, u_2, u_3]

    relay_wait(0)
    wait_halo(4)
    wait_halo(5)
    for t in range(last + 1):
        fill_extra(t + 1, ok_mid, col_recv[0, 1], col_recv[1, 1], t)
    for i in range(rows):
        tile = 0 if i < per else 2
        fill_kap(HALO + i, ok_mid, col_recv[0, tile], col_recv[1, tile], i % per)

    def row_of(p, i):
        return frame[p, i + 4 : i + 5, :]

    def advance(s, i):
        new = step(states[s], i)
        if s < STEPS - 1:
            states[s + 1][i] = new
        else:
            field[8 * (i - HALO) : 8 * (i - HALO) + 8, :] = new[:, 0:cols]

    for i in range(HALO, HALO + rows):
        u_0[i] = jnp.broadcast_to(row_of(0, i), (8, cext))
    for i in range(HALO + 1, HALO + rows - 1):
        coefficients(i, ok_mid, row_of(1, i), row_of(2, i))
    relay_wait(1)
    for s in range(STEPS):
        for i in range(HALO + s + 1, HALO + rows - s - 1):
            advance(s, i)

    sens = sens_v[0]
    n_s = sens.shape[1]
    s_col = sens & (cols - 1)
    s_row = jnp.broadcast_to(sens >> (cols.bit_length() - 1), (8, n_s))
    hot_c = jnp.where(
        lax.broadcasted_iota(jnp.int32, (cols, n_s), 0) == s_col, 1.0, 0.0
    ).astype(jnp.bfloat16)

    def sensed(first_row, count, acc):
        f = field[8 * first_row : 8 * (first_row + count), :]
        f_hi, f_lo = split_bf16(f)
        f_lo2 = ((f - f_hi.astype(jnp.float32)) - f_lo.astype(jnp.float32)).astype(jnp.bfloat16)
        at = dot32(f_hi, hot_c) + (dot32(f_lo, hot_c) + dot32(f_lo2, hot_c))
        for j in range(count):
            acc = jnp.where(s_row == first_row + j, at[8 * j : 8 * j + 8], acc)
        return acc

    own = sensed(8, rows - 16, jnp.zeros((mem, n_s), jnp.float32))

    for k in (0, 1, 2, 3, 6, 7, 8, 9):
        wait_halo(k)
    fill_extra(0, ok_top, corner_recv[2, 0], corner_recv[3, 0], last)
    fill_extra(last + 2, ok_bot, corner_recv[0, 1], corner_recv[1, 1], 0)
    for k in range(HALO):
        fill_kap(k, ok_top, corner_recv[2, 1], corner_recv[3, 1], per - HALO + k)
        fill_kap(HALO + rows + k, ok_bot, corner_recv[0, 0], corner_recv[1, 0], k)

    for k in range(HALO):
        u_0[k] = jnp.broadcast_to(row_of(0, k), (8, cext))
        i = HALO + rows + k
        u_0[i] = jnp.broadcast_to(row_of(0, i), (8, cext))
    for i in range(1, HALO + 1):
        j = 2 * HALO + rows - 1 - i
        coefficients(i, ok_top if i < HALO else ok_mid, row_of(1, i), row_of(2, i))
        coefficients(j, ok_bot if i < HALO else ok_mid, row_of(1, j), row_of(2, j))
    for s in range(STEPS):
        for i in range(1 + s, HALO + 1 + s):
            j = 2 * HALO + rows - 1 - i
            advance(s, i)
            advance(s, j)
    own = sensed(0, 8, own)
    own = sensed(rows - 8, 8, own)
    mine = pl.ds(pl.multiple_of(e * mem, mem), mem)
    preds[mine, :] = own
    for m in range(mem):
        pred[m, 0] = own[m : m + 1]

    def spread(src, dst, ssem, rsem, ids):
        copies = []
        for d, device in enumerate(ids):
            copies.append(send(src, dst, ssem.at[d], rsem.at[d], device))
        return copies

    relay_wait(2)
    copies = spread(preds.at[mine], preds.at[mine], pred_ssem, pred_rsem, ens_ids)
    for copy in copies:
        copy.wait_recv()

    flat = preds[...]
    mean = jnp.sum(flat, axis=0, keepdims=True) * (1.0 / (n_e * mem))
    inv_noise = 1.0 / noise_v[0]
    weighted = (flat - mean) * inv_noise
    miss = (targ_v[0] - mean) * inv_noise
    members = n_e * mem
    against = jnp.concatenate(
        [weighted, miss, jnp.zeros((LANES - members - 1, n_s), jnp.float32)], axis=0
    )
    gram = lax.dot_general(
        preds[mine, :] - mean, against, (((1,), (1,)), ((), ())),
        precision=lax.Precision.HIGHEST, preferred_element_type=jnp.float32,
    )

    zbuf[z] = gram
    copies = spread(zbuf.at[z], zbuf.at[z], z_ssem, z_rsem, z_ids)

    def recv_half(slot, index, h):
        remote(part(index, h), part(index, h), th_ssem.at[slot], th_rsem.at[slot], to_o).wait_recv()

    near_l, near_r, far = x_l * 2 + core, x_r * 2 + core, x_f * 2 + core
    recv_half(0, near_l, 0)
    send_half(near_l, 0, 6, to_r)
    recv_half(3, near_r, 1)
    send_half(near_r, 1, 7, to_l)
    recv_half(1, near_l, 1)
    recv_half(2, near_r, 0)
    for h in range(2):
        send_half(near_l, h, 8 + h, to_o)
        send_half(near_r, h, 10 + h, to_o)

    for copy in copies:
        copy.wait_recv()
    ybuf[x, y] = jnp.sum(zbuf[...], axis=0)
    copies = spread(ybuf.at[x, y], ybuf.at[x, y], y_ssem, y_rsem, y_ids)

    def halves(index):
        at = pl.ds(pl.multiple_of(index * mem * 8, mem * 8), mem * 8)
        for t in range(rows // 8):
            hi, lo = split_bf16(blocks[index, :, 8 * t : 8 * t + 8, :].reshape(mem * 8, cols))
            th_hi[t, at, :] = hi
            th_lo[t, at, :] = lo

    other = x * 2 + 1 - core
    for index in (e, near_l, near_r):
        halves(index)
    recv_half(4, other, 0)
    recv_half(5, other, 1)
    halves(other)
    recv_half(6, far, 0)
    send_half(far, 0, 12, to_o)
    recv_half(7, far, 1)
    send_half(far, 1, 13, to_o)
    halves(far)
    for copy in copies:
        copy.wait_recv()
    gall[core] = jnp.sum(ybuf[...], axis=1)
    copies = [send(gall.at[core], gall.at[core], g_ssem.at[0], g_rsem.at[0], to_o)]

    for h in range(2):
        recv_half(8 + h, x_l * 2 + 1 - core, h)
        recv_half(10 + h, x_r * 2 + 1 - core, h)
        recv_half(12 + h, x_f * 2 + 1 - core, h)
    for other in (x_l, x_r, x_f):
        halves(other * 2 + 1 - core)
    for copy in copies:
        copy.wait_recv()

    arow = lax.broadcasted_iota(jnp.int32, (members, LANES), 0)
    acol = lax.broadcasted_iota(jnp.int32, (members, LANES), 1)
    first = members + 8
    unit = (arow == acol) | ((acol >= first) & (acol < first + mem) & (acol - first == arow - e * mem))
    sums = jnp.concatenate([gall[i % 2, i // 2] for i in range(n_e)], axis=0)
    aug = sums * (1.0 / (members - 1)) + jnp.where(unit, 1.0, 0.0)
    aug = eliminate(aug, members, 8)
    weight = aug[:, first : first + mem] + aug[:, members : members + 1]

    wide = members * 8
    pick = jnp.where(
        lax.broadcasted_iota(jnp.int32, (members, wide), 0)
        == lax.broadcasted_iota(jnp.int32, (members, wide), 1) // 8,
        1.0, 0.0,
    )
    spread_w = lax.dot_general(
        weight, pick, (((0,), (0,)), ((), ())),
        precision=lax.Precision.HIGHEST, preferred_element_type=jnp.float32,
    )
    big = jnp.broadcast_to(spread_w[:, None, :], (mem, 8, wide)).reshape(mem * 8, wide)
    same = (
        lax.broadcasted_iota(jnp.int32, (mem * 8, wide), 0) % 8
        == lax.broadcasted_iota(jnp.int32, (mem * 8, wide), 1) % 8
    )
    big = jnp.where(same, big, 0.0)
    b_hi, b_lo = split_bf16(big)
    b_both = jnp.concatenate([b_hi, b_lo], axis=0)

    outs = []
    for t in range(rows // 8):
        two = dot32(b_both, th_hi[t])
        new = two[: mem * 8] + (dot32(b_hi, th_lo[t]) + two[mem * 8 :])
        result[:, 8 * t : 8 * t + 8, :] = new.reshape(mem, 8, cols)
        copy = pltpu.make_async_copy(
            result.at[:, pl.ds(8 * t, 8)], out.at[:, pl.ds(8 * t, 8)], out_sem.at[t]
        )
        copy.start()
        outs.append(copy)
    for copy, there, _ in halo_copies:
        pl.when(there)(copy.wait_send)
    for copy in sends:
        copy.wait_send()
    for copy in outs:
        copy.wait()


def shards(sizes, theta, initial, velocity, sensors, target, noise):
    mem, rows, cols = theta.shape
    n_s = sensors.shape[-1]
    n_e, n_r, n_c, n_z = sizes
    n_y = n_r // n_z * n_c
    members = n_e * mem
    rext, cext = rows + 2 * HALO, cols + LANES
    f32 = jnp.float32
    DMA = pltpu.SemaphoreType.DMA
    return pl.pallas_call(
        functools.partial(kernel, sizes),
        out_shape=(
            jax.ShapeDtypeStruct(theta.shape, f32),
            jax.ShapeDtypeStruct((mem, 1, 1, n_s), f32),
        ),
        in_specs=[pl.BlockSpec(memory_space=pltpu.HBM)] * 6,
        out_specs=(pl.BlockSpec(memory_space=pltpu.HBM), pl.BlockSpec(memory_space=pltpu.VMEM)),
        scratch_shapes=[
            pltpu.VMEM((n_e, mem, rows, cols), f32),
            pltpu.VMEM((rext, mem, cols), f32),
            pltpu.VMEM((3, rows + 16, cols), f32),
            pltpu.VMEM((3, rows + 16, cext), f32),
            pltpu.VMEM((1, 1, n_s), jnp.int32),
            pltpu.VMEM((1, 1, n_s), f32),
            pltpu.VMEM((1, 1, n_s), f32),
            pltpu.VMEM((2, 3, 8, LANES), f32),
            pltpu.VMEM((2, 3, 8, LANES), f32),
            pltpu.VMEM((4, 2, 8, LANES), f32),
            *[pltpu.VMEM((rext, mem, cext), f32)] * 10,
            pltpu.VMEM((mem * rows, cols), f32),
            pltpu.VMEM((members, n_s), f32),
            pltpu.VMEM((n_z, mem, LANES), f32),
            pltpu.VMEM((n_e // 2, n_y, mem, LANES), f32),
            pltpu.VMEM((2, n_e // 2, mem, LANES), f32),
            pltpu.VMEM((rows // 8, members * 8, cols), jnp.bfloat16),
            pltpu.VMEM((rows // 8, members * 8, cols), jnp.bfloat16),
            pltpu.VMEM((mem, rows, cols), f32),
            DMA((6,)),
            DMA((10,)), DMA((10,)),
            DMA((n_e - 1,)), DMA((n_e - 1,)),
            DMA((n_z - 1,)), DMA((n_z - 1,)),
            DMA((n_e // 2 * n_y - 1,)), DMA((n_e // 2 * n_y - 1,)),
            DMA((1,)), DMA((1,)),
            DMA((14,)), DMA((14,)),
            DMA((rows // 8,)),
            pltpu.SemaphoreType.REGULAR((3,)),
        ],
        compiler_params=pltpu.CompilerParams(
            collective_id=0, has_side_effects=True, vmem_limit_bytes=48 * 1024 * 1024
        ),
    )(*(pltpu.with_memory_space_constraint(a, pltpu.HBM)
        for a in (theta, initial, velocity, sensors, target, noise)))


def solution(mesh):
    in_specs = (
        P("ens", "row", "col"),
        P("row", "col"),
        P(None, "row", "col"),
        P("row", "col", None),
        P("row", "col", None),
        P("row", "col", None),
    )
    out_specs = (P("ens", "row", "col"), P("ens", "row", "col", None))
    n_r = mesh.shape["row"]
    sizes = (mesh.shape["ens"], n_r, mesh.shape["col"], n_r // 2)
    return jax.shard_map(
        functools.partial(shards, sizes),
        mesh=mesh, in_specs=in_specs, out_specs=out_specs, check_vma=False,
    )
```

```python
import functools

import jax
import jax.numpy as jnp
from jax import lax
from jax.experimental import pallas as pl
from jax.experimental.pallas import tpu as pltpu
from jax.sharding import PartitionSpec as P

STEPS = 4
diffuse_rate = 0.07
advect_rate = 0.3

MESH = pl.DeviceIdType.MESH
HALO = 4
LANES = 128


def roll(x, shift, axis):
    shift = shift % x.shape[axis]
    return x if shift == 0 else pltpu.roll(x, shift, axis)


def split_bf16(x):
    hi = x.astype(jnp.bfloat16)
    lo = (x - hi.astype(jnp.float32)).astype(jnp.bfloat16)
    return hi, lo


def dot32(a, b):
    return jnp.dot(a, b, preferred_element_type=jnp.float32)


def eliminate(aug, n, p):
    arow = lax.broadcasted_iota(jnp.int32, aug.shape, 0)
    for k in range(0, n, p):
        col = [jnp.broadcast_to(aug[:, k + j : k + j + 1], aug.shape) for j in range(p)]
        d = [[col[j][k + i : k + i + 1, :] for j in range(p)] for i in range(p)]
        new = [aug[k + i : k + i + 1, :] for i in range(p)]
        for i in range(p):
            inv = 1.0 / d[i][i]
            for j in range(i + 1, p):
                d[i][j] = d[i][j] * inv
            new[i] = new[i] * inv
            for q in range(p):
                if q != i:
                    for j in range(i + 1, p):
                        d[q][j] = d[q][j] - d[q][i] * d[i][j]
                    new[q] = new[q] - d[q][i] * new[i]
        less = col[0] * new[0]
        for j in range(1, p):
            less = less + col[j] * new[j]
        aug = aug - less
        for j in range(p):
            aug = jnp.where(arow == k + j, new[j], aug)
    return aug


def kernel(
    sizes,
    theta, initial, velocity, sensors, target, noise,
    out, pred,
    blocks, logk, extra, frame, sens_v, targ_v, noise_v,
    col_send, col_recv, corner_recv,
    kap, c_0, c_u, c_d, c_r, c_l, u_0, u_1, u_2, u_3, field,
    preds, zbuf, ybuf, gall, th_hi, th_lo, result,
    load_sem, halo_ssem, halo_rsem, pred_ssem, pred_rsem,
    z_ssem, z_rsem, y_ssem, y_rsem, g_ssem, g_rsem,
    th_ssem, th_rsem, out_sem, relay_sem,
):
    n_e, n_r, n_c, n_z = sizes
    n_x = n_e // 2
    n_yh = n_r // n_z
    n_y = n_yh * n_c
    mem, rows, cols = theta.shape
    cext = cols + LANES
    e, r, c = lax.axis_index("ens"), lax.axis_index("row"), lax.axis_index("col")
    x, core = e // 2, e % 2
    yh, z = r // n_z, r % n_z
    y = yh * n_c + c

    loads = [
        pltpu.make_async_copy(theta, blocks.at[e], load_sem.at[0]),
        pltpu.make_async_copy(initial, extra.at[0, pl.ds(8, rows)], load_sem.at[1]),
        pltpu.make_async_copy(
            velocity, extra.at[pl.ds(1, 2), pl.ds(8, rows)], load_sem.at[2]
        ),
        pltpu.make_async_copy(sensors, sens_v, load_sem.at[3]),
        pltpu.make_async_copy(target, targ_v, load_sem.at[4]),
        pltpu.make_async_copy(noise, noise_v, load_sem.at[5]),
    ]
    for copy in loads:
        copy.start()

    prev, nxt = (r + n_r - 1) % n_r, (r + 1) % n_r
    left, right = (c + n_c - 1) % n_c, (c + 1) % n_c
    halo_ids = [
        {"row": prev}, {"row": nxt}, {"col": left}, {"col": right},
        {"row": prev, "col": left}, {"row": prev, "col": right},
        {"row": nxt, "col": left}, {"row": nxt, "col": right},
    ]
    ens_ids = [{"ens": (e + d) % n_e} for d in range(1, n_e)]
    z_ids = [{"row": yh * n_z + (z + d) % n_z} for d in range(1, n_z)]
    y_ids = []
    for d in range(1, n_y):
        other = (y + d) % n_y
        y_ids.append({"row": other // n_c * n_z + z, "col": other % n_c})

    has_p, has_n, has_l, has_r = r > 0, r < n_r - 1, c > 0, c < n_c - 1
    halo_out = [
        has_p, has_n, has_l, has_r, has_p & has_l, has_p & has_r, has_n & has_l, has_n & has_r
    ]
    halo_in = [
        has_n, has_p, has_r, has_l, has_n & has_r, has_n & has_l, has_p & has_r, has_p & has_l
    ]
    x_r, x_l, x_f = (x + 1) % n_x, (x + n_x - 1) % n_x, (x + 2) % n_x
    to_r, to_l = {"ens": x_r * 2 + core}, {"ens": x_l * 2 + core}
    to_o = {"ens": x * 2 + (1 - core)}
    y_r, y_l = (y + 1) % n_y, (y + n_y - 1) % n_y
    near_ids = [
        to_r, to_l, to_o,
        {"row": yh * n_z + (z + 1) % n_z}, {"row": yh * n_z + (z + n_z - 1) % n_z},
        {"row": y_r // n_c * n_z + z, "col": y_r % n_c},
        {"row": y_l // n_c * n_z + z, "col": y_l % n_c},
    ]

    barrier = pltpu.get_barrier_semaphore()
    for device in near_ids:
        pl.semaphore_signal(barrier, inc=1, device_id=device, device_id_type=MESH)
    for device, there in zip(halo_ids, halo_out, strict=True):
        @pl.when(there)
        def _(device=device):
            pl.semaphore_signal(barrier, inc=1, device_id=device, device_id_type=MESH)
    one = [jnp.where(v, 1, 0) for v in (has_p, has_n, has_l, has_r)]
    n_halo = (1 + one[0] + one[1]) * (1 + one[2] + one[3]) - 1
    pl.semaphore_wait(barrier, len(near_ids) + n_halo)

    def relay_signal(j):
        for device in near_ids:
            pl.semaphore_signal(
                relay_sem.at[j], inc=1, device_id=device, device_id_type=MESH
            )

    def relay_wait(j):
        pl.semaphore_wait(relay_sem.at[j], len(near_ids))
        if j < 2:
            relay_signal(j + 1)

    relay_signal(0)
    sends = []

    def remote(src, dst, ssem, rsem, device):
        copy = pltpu.make_async_remote_copy(
            src_ref=src, dst_ref=dst, send_sem=ssem, recv_sem=rsem,
            device_id=device, device_id_type=MESH,
        )
        return copy

    def send(*args):
        copy = remote(*args)
        copy.start()
        sends.append(copy)
        return copy

    for copy in loads:
        copy.wait()

    half = mem // 2

    def part(index, h):
        return blocks.at[index, pl.ds(h * half, half)]

    def send_half(index, h, slot, device):
        return send(part(index, h), part(index, h), th_ssem.at[slot], th_rsem.at[slot], device)

    send_half(e, 0, 0, to_r)
    send_half(e, 1, 3, to_l)
    for h in range(2):
        send_half(e, h, 4 + h, to_o)

    def turned(t):
        tile = blocks[e, :, 8 * t : 8 * t + 8, :]
        logk[HALO + 8 * t : HALO + 8 * t + 8] = jnp.swapaxes(tile, 0, 1)

    last = rows // 8 - 1
    turned(0)
    turned(last)

    halo_copies = []

    def send_halo(k, src, dst, which):
        copy = remote(src, dst, halo_ssem.at[k], halo_rsem.at[k], halo_ids[which])
        pl.when(halo_out[which])(copy.start)
        halo_copies.append((copy, halo_out[which], halo_in[which]))

    def wait_halo(k):
        copy, _, there = halo_copies[k]
        pl.when(there)(copy.wait_recv)

    def edge(start):
        return logk.at[pl.ds(start, HALO)]

    def edge_x(start):
        return extra.at[:, pl.ds(start, 8)]

    send_halo(0, edge(HALO), edge(rows + HALO), 0)
    send_halo(1, edge(rows), edge(0), 1)
    send_halo(2, edge_x(8), edge_x(rows + 8), 0)
    send_halo(3, edge_x(rows), edge_x(0), 1)
    for t in range(1, last):
        turned(t)

    lane = lax.broadcasted_iota(jnp.int32, (8, LANES), 1)
    slot_of = lane // HALO
    per = LANES // HALO
    for side in range(2):
        low = 0 if side == 0 else cols - LANES
        off = 0 if side == 0 else HALO
        for half_t, first_row in ((0, 0), (2, per)):
            acc = jnp.zeros((8, LANES), jnp.float32)
            for k in range(per):
                row = logk[HALO + first_row + k, :, low : low + LANES]
                acc = jnp.where(slot_of == k, roll(row, HALO * k + off, 1), acc)
            col_send[side, half_t] = acc
        acc = jnp.zeros((8, LANES), jnp.float32)
        for p in range(3):
            for t in range(last + 1):
                k = p * (last + 1) + t
                row = extra[p, 8 + 8 * t : 16 + 8 * t, low : low + LANES]
                acc = jnp.where(slot_of == k, roll(row, HALO * k + off, 1), acc)
        col_send[side, 1] = acc
        send_halo(4 + side, col_send.at[side], col_recv.at[side], 2 + side)
    for k in range(4):
        part_k = pl.ds(0 if k < 2 else 1, 2)
        send_halo(6 + k, col_send.at[k % 2, part_k], corner_recv.at[k], 4 + k)

    ci = lax.broadcasted_iota(jnp.int32, (8, cext), 1)
    c_lo = jnp.where(c < n_c - 1, cols + HALO, cols)
    c_hi = jnp.where(c > 0, cext - HALO, cext)
    ok_mid = (ci < c_lo) | (ci >= c_hi)
    ok_top = ok_mid & (r > 0)
    ok_bot = ok_mid & (r < n_r - 1)
    near = lane < LANES // 2
    half_d, half_a = 0.5 * diffuse_rate, 0.5 * advect_rate

    def unpack(from_right, from_left, k):
        return jnp.where(near, roll(from_right, -HALO * k, 1), roll(from_left, -HALO - HALO * k, 1))

    def fill_kap(i, ok, from_right, from_left, k):
        kap[i, :, 0:cols] = jnp.where(ok[:, 0:cols], half_d * jnp.exp(logk[i]), 0.0)
        outer = unpack(from_right, from_left, k)
        kap[i, :, cols:cext] = jnp.where(ok[:, cols:cext], half_d * jnp.exp(outer), 0.0)

    def fill_extra(t, ok, from_right, from_left, slot_t):
        at = slice(8 * t, 8 * t + 8)
        for p in range(3):
            scale = 1.0 if p == 0 else half_a
            outer = unpack(from_right, from_left, p * (last + 1) + slot_t)
            frame[p, at, 0:cols] = jnp.where(ok[:, 0:cols], scale * extra[p, at], 0.0)
            frame[p, at, cols:cext] = jnp.where(ok[:, cols:cext], scale * outer, 0.0)

    def coefficients(i, ok, v0, v1):
        k = kap[i]
        f_u, f_d = k + kap[i + 1], k + kap[i - 1]
        f_r, f_l = k + roll(k, -1, 1), k + roll(k, 1, 1)
        c_0[i] = jnp.where(ok, 1.0 - ((f_u + f_d) + (f_r + f_l)), 0.0)
        c_u[i] = jnp.where(ok, f_u - v0, 0.0)
        c_d[i] = jnp.where(ok, f_d + v0, 0.0)
        c_r[i] = jnp.where(ok, f_r - v1, 0.0)
        c_l[i] = jnp.where(ok, f_l + v1, 0.0)

    def step(src, i):
        u = src[i]
        return (
            c_0[i] * u
            + (c_u[i] * src[i + 1] + c_d[i] * src[i - 1])
            + (c_r[i] * roll(u, -1, 1) + c_l[i] * roll(u, 1, 1))
        )

    states = [u_0, u_1, u_2, u_3]

    relay_wait(0)
    wait_halo(4)
    wait_halo(5)
    for t in range(last + 1):
        fill_extra(t + 1, ok_mid, col_recv[0, 1], col_recv[1, 1], t)
    for i in range(rows):
        tile = 0 if i < per else 2
        fill_kap(HALO + i, ok_mid, col_recv[0, tile], col_recv[1, tile], i % per)

    def row_of(p, i):
        return frame[p, i + 4 : i + 5, :]

    def advance(s, i):
        new = step(states[s], i)
        if s < STEPS - 1:
            states[s + 1][i] = new
        else:
            field[8 * (i - HALO) : 8 * (i - HALO) + 8, :] = new[:, 0:cols]

    for i in range(HALO, HALO + rows):
        u_0[i] = jnp.broadcast_to(row_of(0, i), (8, cext))
    for i in range(HALO + 1, HALO + rows - 1):
        coefficients(i, ok_mid, row_of(1, i), row_of(2, i))
    relay_wait(1)
    for s in range(STEPS):
        for i in range(HALO + s + 1, HALO + rows - s - 1):
            advance(s, i)

    sens = sens_v[0]
    n_s = sens.shape[1]
    s_col = sens & (cols - 1)
    s_row = jnp.broadcast_to(sens >> (cols.bit_length() - 1), (8, n_s))
    hot_c = jnp.where(
        lax.broadcasted_iota(jnp.int32, (cols, n_s), 0) == s_col, 1.0, 0.0
    ).astype(jnp.bfloat16)

    def sensed(first_row, count, acc):
        f = field[8 * first_row : 8 * (first_row + count), :]
        f_hi, f_lo = split_bf16(f)
        f_lo2 = ((f - f_hi.astype(jnp.float32)) - f_lo.astype(jnp.float32)).astype(jnp.bfloat16)
        at = dot32(f_hi, hot_c) + (dot32(f_lo, hot_c) + dot32(f_lo2, hot_c))
        for j in range(count):
            acc = jnp.where(s_row == first_row + j, at[8 * j : 8 * j + 8], acc)
        return acc

    own = sensed(8, rows - 16, jnp.zeros((mem, n_s), jnp.float32))

    for k in (0, 1, 2, 3, 6, 7, 8, 9):
        wait_halo(k)
    fill_extra(0, ok_top, corner_recv[2, 0], corner_recv[3, 0], last)
    fill_extra(last + 2, ok_bot, corner_recv[0, 1], corner_recv[1, 1], 0)
    for k in range(HALO):
        fill_kap(k, ok_top, corner_recv[2, 1], corner_recv[3, 1], per - HALO + k)
        fill_kap(HALO + rows + k, ok_bot, corner_recv[0, 0], corner_recv[1, 0], k)

    for k in range(HALO):
        u_0[k] = jnp.broadcast_to(row_of(0, k), (8, cext))
        i = HALO + rows + k
        u_0[i] = jnp.broadcast_to(row_of(0, i), (8, cext))
    for i in range(1, HALO + 1):
        j = 2 * HALO + rows - 1 - i
        coefficients(i, ok_top if i < HALO else ok_mid, row_of(1, i), row_of(2, i))
        coefficients(j, ok_bot if i < HALO else ok_mid, row_of(1, j), row_of(2, j))
    for s in range(STEPS):
        for i in range(1 + s, HALO + 1 + s):
            j = 2 * HALO + rows - 1 - i
            advance(s, i)
            advance(s, j)
    own = sensed(0, 8, own)
    own = sensed(rows - 8, 8, own)
    mine = pl.ds(pl.multiple_of(e * mem, mem), mem)
    preds[mine, :] = own
    for m in range(mem):
        pred[m, 0] = own[m : m + 1]

    def spread(src, dst, ssem, rsem, ids):
        copies = []
        for d, device in enumerate(ids):
            copies.append(send(src, dst, ssem.at[d], rsem.at[d], device))
        return copies

    copies = spread(preds.at[mine], preds.at[mine], pred_ssem, pred_rsem, ens_ids)
    relay_wait(2)

    def recv_half(slot, index, h):
        remote(part(index, h), part(index, h), th_ssem.at[slot], th_rsem.at[slot], to_o).wait_recv()

    near_l, near_r, far = x_l * 2 + core, x_r * 2 + core, x_f * 2 + core
    other = x * 2 + 1 - core
    recv_half(0, near_l, 0)
    recv_half(3, near_r, 1)
    for copy in copies:
        copy.wait_recv()

    send_half(e, 1, 1, to_r)
    send_half(e, 0, 2, to_l)
    send_half(near_l, 0, 6, to_r)
    send_half(near_r, 1, 7, to_l)

    flat = preds[...]
    members = n_e * mem
    hm, qm = members // 2, members // 4
    mean = jnp.sum(flat, axis=0, keepdims=True) * (1.0 / members)
    inv_noise = 1.0 / noise_v[0]
    against = jnp.where(
        lax.broadcasted_iota(jnp.int32, (members, n_s), 0) == members - 1,
        targ_v[0] - mean, flat - mean,
    ) * inv_noise
    gram = lax.dot_general(
        preds[pl.ds(pl.multiple_of(core * hm, hm), hm), :] - mean, against,
        (((1,), (1,)), ((), ())),
        precision=lax.Precision.HIGHEST, preferred_element_type=jnp.float32,
    )
    zbuf[z] = jnp.concatenate([gram[:qm], gram[qm:]], axis=1)
    copies = spread(zbuf.at[z], zbuf.at[z], z_ssem, z_rsem, z_ids)

    def halves(index, slot):
        at = slice(slot * mem * 8, (slot + 1) * mem * 8)
        for t in range(rows // 8):
            hi, lo = split_bf16(blocks[index, :, 8 * t : 8 * t + 8, :].reshape(mem * 8, cols))
            th_hi[t, at, :] = hi
            th_lo[t, at, :] = lo

    halves(e, 0)
    recv_half(4, other, 0)
    recv_half(5, other, 1)
    halves(other, 1)
    send_half(near_l, 0, 8, to_o)
    send_half(near_r, 1, 11, to_o)
    for copy in copies:
        copy.wait_recv()

    ybuf[y] = jnp.sum(zbuf[...], axis=0)
    copies = spread(ybuf.at[y], ybuf.at[y], y_ssem, y_rsem, y_ids)
    recv_half(1, near_l, 1)
    recv_half(2, near_r, 0)
    send_half(near_l, 1, 9, to_o)
    send_half(near_r, 0, 10, to_o)
    halves(near_l, 2)
    halves(near_r, 4)
    for copy in copies:
        copy.wait_recv()
    gall[core] = jnp.sum(ybuf[...], axis=0)
    copies = [send(gall.at[core], gall.at[core], g_ssem.at[0], g_rsem.at[0], to_o)]
    for h in range(2):
        recv_half(8 + h, x_l * 2 + 1 - core, h)
        recv_half(10 + h, x_r * 2 + 1 - core, h)
    halves(x_l * 2 + 1 - core, 3)
    halves(x_r * 2 + 1 - core, 5)
    for copy in copies:
        copy.wait_recv()

    arow = lax.broadcasted_iota(jnp.int32, (members, LANES), 0)
    acol = lax.broadcasted_iota(jnp.int32, (members, LANES), 1)
    first = members + 8
    unit = (arow == acol) | ((acol >= first) & (acol < first + mem) & (acol - first == arow - e * mem))
    quarters = [gall[q][:, w : w + members] for q in range(2) for w in (0, members)]
    sums = jnp.concatenate(quarters, axis=0)
    sums = jnp.concatenate([sums, jnp.zeros_like(sums)], axis=1)
    others = jnp.sum(jnp.where(acol < members - 1, sums, 0.0), axis=1, keepdims=True)
    sums = jnp.where(
        acol == members - 1, -others,
        jnp.where(acol == members, sums[:, members - 1 : members], sums),
    )
    aug = sums * (1.0 / (members - 1)) + jnp.where(unit, 1.0, 0.0)
    aug = eliminate(aug, members, 8)
    weight = aug[:, first : first + mem] + aug[:, members : members + 1]

    wide = members * 8
    col_id = lax.broadcasted_iota(jnp.int32, (members, wide), 1)
    slots = [e, other]
    for chip in (x_l, x_r, x_f):
        slots += [chip * 2 + core, chip * 2 + 1 - core]
    k_of = (col_id // 8) % mem
    for i, index in enumerate(slots):
        k_of = jnp.where(col_id // (8 * mem) == i, k_of + index * mem, k_of)
    pick = jnp.where(lax.broadcasted_iota(jnp.int32, (members, wide), 0) == k_of, 1.0, 0.0)
    spread_w = lax.dot_general(
        weight, pick, (((0,), (0,)), ((), ())),
        precision=lax.Precision.HIGHEST, preferred_element_type=jnp.float32,
    )
    big = jnp.broadcast_to(spread_w[:, None, :], (mem, 8, wide)).reshape(mem * 8, wide)
    same = (
        lax.broadcasted_iota(jnp.int32, (mem * 8, wide), 0) % 8
        == lax.broadcasted_iota(jnp.int32, (mem * 8, wide), 1) % 8
    )
    big = jnp.where(same, big, 0.0)
    b_hi, b_lo = split_bf16(big)
    b_both = jnp.concatenate([b_hi, b_lo], axis=0)

    def product(t, lo, hi):
        two = dot32(b_both[:, lo:hi], th_hi[t, lo:hi, :])
        return two[: mem * 8] + (dot32(b_hi[:, lo:hi], th_lo[t, lo:hi, :]) + two[mem * 8 :])

    recv_half(6, far, 0)
    send_half(far, 0, 12, to_o)
    recv_half(7, far, 1)
    send_half(far, 1, 13, to_o)
    cut = wide - 2 * mem * 8
    for t in range(rows // 8):
        result[:, 8 * t : 8 * t + 8, :] = product(t, 0, cut).reshape(mem, 8, cols)
    halves(far, 6)
    recv_half(12, x_f * 2 + 1 - core, 0)
    recv_half(13, x_f * 2 + 1 - core, 1)
    halves(x_f * 2 + 1 - core, 7)
    outs = []
    for t in range(rows // 8):
        result[:, 8 * t : 8 * t + 8, :] += product(t, cut, wide).reshape(mem, 8, cols)
        copy = pltpu.make_async_copy(
            result.at[:, pl.ds(8 * t, 8)], out.at[:, pl.ds(8 * t, 8)], out_sem.at[t]
        )
        copy.start()
        outs.append(copy)
    for copy, there, _ in halo_copies:
        pl.when(there)(copy.wait_send)
    for copy in sends:
        copy.wait_send()
    for copy in outs:
        copy.wait()


def shards(sizes, theta, initial, velocity, sensors, target, noise):
    mem, rows, cols = theta.shape
    n_s = sensors.shape[-1]
    n_e, n_r, n_c, n_z = sizes
    n_y = n_r // n_z * n_c
    members = n_e * mem
    rext, cext = rows + 2 * HALO, cols + LANES
    f32 = jnp.float32
    DMA = pltpu.SemaphoreType.DMA
    return pl.pallas_call(
        functools.partial(kernel, sizes),
        out_shape=(
            jax.ShapeDtypeStruct(theta.shape, f32),
            jax.ShapeDtypeStruct((mem, 1, 1, n_s), f32),
        ),
        in_specs=[pl.BlockSpec(memory_space=pltpu.HBM)] * 6,
        out_specs=(pl.BlockSpec(memory_space=pltpu.HBM), pl.BlockSpec(memory_space=pltpu.VMEM)),
        scratch_shapes=[
            pltpu.VMEM((n_e, mem, rows, cols), f32),
            pltpu.VMEM((rext, mem, cols), f32),
            pltpu.VMEM((3, rows + 16, cols), f32),
            pltpu.VMEM((3, rows + 16, cext), f32),
            pltpu.VMEM((1, 1, n_s), jnp.int32),
            pltpu.VMEM((1, 1, n_s), f32),
            pltpu.VMEM((1, 1, n_s), f32),
            pltpu.VMEM((2, 3, 8, LANES), f32),
            pltpu.VMEM((2, 3, 8, LANES), f32),
            pltpu.VMEM((4, 2, 8, LANES), f32),
            *[pltpu.VMEM((rext, mem, cext), f32)] * 10,
            pltpu.VMEM((mem * rows, cols), f32),
            pltpu.VMEM((members, n_s), f32),
            pltpu.VMEM((n_z, members // 4, LANES), f32),
            pltpu.VMEM((n_y, members // 4, LANES), f32),
            pltpu.VMEM((2, members // 4, LANES), f32),
            pltpu.VMEM((rows // 8, members * 8, cols), jnp.bfloat16),
            pltpu.VMEM((rows // 8, members * 8, cols), jnp.bfloat16),
            pltpu.VMEM((mem, rows, cols), f32),
            DMA((6,)),
            DMA((10,)), DMA((10,)),
            DMA((n_e - 1,)), DMA((n_e - 1,)),
            DMA((n_z - 1,)), DMA((n_z - 1,)),
            DMA((n_y - 1,)), DMA((n_y - 1,)),
            DMA((1,)), DMA((1,)),
            DMA((14,)), DMA((14,)),
            DMA((rows // 8,)),
            pltpu.SemaphoreType.REGULAR((3,)),
        ],
        compiler_params=pltpu.CompilerParams(
            collective_id=0, has_side_effects=True, vmem_limit_bytes=48 * 1024 * 1024
        ),
    )(*(pltpu.with_memory_space_constraint(a, pltpu.HBM)
        for a in (theta, initial, velocity, sensors, target, noise)))


def solution(mesh):
    in_specs = (
        P("ens", "row", "col"),
        P("row", "col"),
        P(None, "row", "col"),
        P("row", "col", None),
        P("row", "col", None),
        P("row", "col", None),
    )
    out_specs = (P("ens", "row", "col"), P("ens", "row", "col", None))
    n_r = mesh.shape["row"]
    sizes = (mesh.shape["ens"], n_r, mesh.shape["col"], n_r // 2)
    return jax.shard_map(
        functools.partial(shards, sizes),
        mesh=mesh, in_specs=in_specs, out_specs=out_specs, check_vma=False,
    )
```

```python
import functools

import jax
import jax.numpy as jnp
from jax import lax
from jax.experimental import pallas as pl
from jax.experimental.pallas import tpu as pltpu
from jax.sharding import PartitionSpec as P

STEPS = 4
diffuse_rate = 0.07
advect_rate = 0.3

MESH = pl.DeviceIdType.MESH
HALO = 4
LANES = 128


def roll(x, shift, axis):
    shift = shift % x.shape[axis]
    return x if shift == 0 else pltpu.roll(x, shift, axis)


def split_bf16(x):
    hi = x.astype(jnp.bfloat16)
    lo = (x - hi.astype(jnp.float32)).astype(jnp.bfloat16)
    return hi, lo


def dot32(a, b):
    return jnp.dot(a, b, preferred_element_type=jnp.float32)


def eliminate(aug, n, p):
    arow = lax.broadcasted_iota(jnp.int32, aug.shape, 0)
    for k in range(0, n, p):
        col = [jnp.broadcast_to(aug[:, k + j : k + j + 1], aug.shape) for j in range(p)]
        d = [[col[j][k + i : k + i + 1, :] for j in range(p)] for i in range(p)]
        new = [aug[k + i : k + i + 1, :] for i in range(p)]
        for i in range(p):
            inv = 1.0 / d[i][i]
            for j in range(i + 1, p):
                d[i][j] = d[i][j] * inv
            new[i] = new[i] * inv
            for q in range(p):
                if q != i:
                    for j in range(i + 1, p):
                        d[q][j] = d[q][j] - d[q][i] * d[i][j]
                    new[q] = new[q] - d[q][i] * new[i]
        less = col[0] * new[0]
        for j in range(1, p):
            less = less + col[j] * new[j]
        aug = aug - less
        for j in range(p):
            aug = jnp.where(arow == k + j, new[j], aug)
    return aug


def kernel(
    sizes,
    theta, initial, velocity, sensors, target, noise,
    out, pred,
    blocks, logk, extra, frame, sens_v, targ_v, noise_v,
    col_send, col_recv, corner_recv,
    kap, c_0, c_u, c_d, c_r, c_l, u_0, u_1, u_2, u_3, field,
    preds, zbuf, ybuf, gall, th_hi, th_lo, result,
    load_sem, halo_ssem, halo_rsem, pred_ssem, pred_rsem,
    z_ssem, z_rsem, y_ssem, y_rsem, g_ssem, g_rsem,
    th_ssem, th_rsem, out_sem, relay_sem,
):
    n_e, n_r, n_c, n_z = sizes
    n_x = n_e // 2
    n_yh = n_r // n_z
    n_y = n_yh * n_c
    mem, rows, cols = theta.shape
    cext = cols + LANES
    e, r, c = lax.axis_index("ens"), lax.axis_index("row"), lax.axis_index("col")
    x, core = e // 2, e % 2
    yh, z = r // n_z, r % n_z
    y = yh * n_c + c

    loads = [
        pltpu.make_async_copy(theta, blocks.at[e], load_sem.at[0]),
        pltpu.make_async_copy(initial, extra.at[0, pl.ds(8, rows)], load_sem.at[1]),
        pltpu.make_async_copy(
            velocity, extra.at[pl.ds(1, 2), pl.ds(8, rows)], load_sem.at[2]
        ),
        pltpu.make_async_copy(sensors, sens_v, load_sem.at[3]),
        pltpu.make_async_copy(target, targ_v, load_sem.at[4]),
        pltpu.make_async_copy(noise, noise_v, load_sem.at[5]),
    ]
    for copy in loads:
        copy.start()

    prev, nxt = (r + n_r - 1) % n_r, (r + 1) % n_r
    left, right = (c + n_c - 1) % n_c, (c + 1) % n_c
    halo_ids = [
        {"row": prev}, {"row": nxt}, {"col": left}, {"col": right},
        {"row": prev, "col": left}, {"row": prev, "col": right},
        {"row": nxt, "col": left}, {"row": nxt, "col": right},
    ]
    ens_ids = [{"ens": (e + d) % n_e} for d in range(1, n_e)]
    z_ids = [{"row": yh * n_z + (z + d) % n_z} for d in range(1, n_z)]
    y_ids = []
    for d in range(1, n_y):
        other = (y + d) % n_y
        y_ids.append({"row": other // n_c * n_z + z, "col": other % n_c})

    has_p, has_n, has_l, has_r = r > 0, r < n_r - 1, c > 0, c < n_c - 1
    halo_out = [
        has_p, has_n, has_l, has_r, has_p & has_l, has_p & has_r, has_n & has_l, has_n & has_r
    ]
    halo_in = [
        has_n, has_p, has_r, has_l, has_n & has_r, has_n & has_l, has_p & has_r, has_p & has_l
    ]
    x_r, x_l, x_f = (x + 1) % n_x, (x + n_x - 1) % n_x, (x + 2) % n_x
    to_r, to_l = {"ens": x_r * 2 + core}, {"ens": x_l * 2 + core}
    to_o = {"ens": x * 2 + (1 - core)}
    y_r, y_l = (y + 1) % n_y, (y + n_y - 1) % n_y
    near_ids = [
        to_r, to_l, to_o,
        {"row": yh * n_z + (z + 1) % n_z}, {"row": yh * n_z + (z + n_z - 1) % n_z},
        {"row": y_r // n_c * n_z + z, "col": y_r % n_c},
        {"row": y_l // n_c * n_z + z, "col": y_l % n_c},
    ]

    barrier = pltpu.get_barrier_semaphore()
    for device in near_ids:
        pl.semaphore_signal(barrier, inc=1, device_id=device, device_id_type=MESH)
    for device, there in zip(halo_ids, halo_out, strict=True):
        @pl.when(there)
        def _(device=device):
            pl.semaphore_signal(barrier, inc=1, device_id=device, device_id_type=MESH)
    def relay_signal(j):
        for device in near_ids:
            pl.semaphore_signal(
                relay_sem.at[j], inc=1, device_id=device, device_id_type=MESH
            )

    def relay_wait(j):
        pl.semaphore_wait(relay_sem.at[j], len(near_ids))
        if j < 2:
            relay_signal(j + 1)

    sends = []

    def remote(src, dst, ssem, rsem, device):
        copy = pltpu.make_async_remote_copy(
            src_ref=src, dst_ref=dst, send_sem=ssem, recv_sem=rsem,
            device_id=device, device_id_type=MESH,
        )
        return copy

    def send(*args):
        copy = remote(*args)
        copy.start()
        sends.append(copy)
        return copy

    for copy in loads:
        copy.wait()

    half = mem // 2

    def part(index, h):
        return blocks.at[index, pl.ds(h * half, half)]

    def send_half(index, h, slot, device):
        return send(part(index, h), part(index, h), th_ssem.at[slot], th_rsem.at[slot], device)

    def turned(t):
        tile = blocks[e, :, 8 * t : 8 * t + 8, :]
        logk[HALO + 8 * t : HALO + 8 * t + 8] = jnp.swapaxes(tile, 0, 1)

    last = rows // 8 - 1
    turned(0)
    turned(last)

    halo_copies = []

    def send_halo(k, src, dst, which):
        copy = remote(src, dst, halo_ssem.at[k], halo_rsem.at[k], halo_ids[which])
        pl.when(halo_out[which])(copy.start)
        halo_copies.append((copy, halo_out[which], halo_in[which]))

    def wait_halo(k):
        copy, _, there = halo_copies[k]
        pl.when(there)(copy.wait_recv)

    def edge(start):
        return logk.at[pl.ds(start, HALO)]

    def edge_x(start):
        return extra.at[:, pl.ds(start, 8)]

    for t in range(1, last):
        turned(t)

    lane = lax.broadcasted_iota(jnp.int32, (8, LANES), 1)
    slot_of = lane // HALO
    per = LANES // HALO
    for side in range(2):
        low = 0 if side == 0 else cols - LANES
        off = 0 if side == 0 else HALO
        for half_t, first_row in ((0, 0), (2, per)):
            acc = jnp.zeros((8, LANES), jnp.float32)
            for k in range(per):
                row = logk[HALO + first_row + k, :, low : low + LANES]
                acc = jnp.where(slot_of == k, roll(row, HALO * k + off, 1), acc)
            col_send[side, half_t] = acc
        acc = jnp.zeros((8, LANES), jnp.float32)
        for p in range(3):
            for t in range(last + 1):
                k = p * (last + 1) + t
                row = extra[p, 8 + 8 * t : 16 + 8 * t, low : low + LANES]
                acc = jnp.where(slot_of == k, roll(row, HALO * k + off, 1), acc)
        col_send[side, 1] = acc
    one = [jnp.where(v, 1, 0) for v in (has_p, has_n, has_l, has_r)]
    n_halo = (1 + one[0] + one[1]) * (1 + one[2] + one[3]) - 1
    pl.semaphore_wait(barrier, len(near_ids) + n_halo)

    relay_signal(0)
    send_halo(0, edge(HALO), edge(rows + HALO), 0)
    send_halo(1, edge(rows), edge(0), 1)
    send_halo(2, edge_x(8), edge_x(rows + 8), 0)
    send_halo(3, edge_x(rows), edge_x(0), 1)
    for side in range(2):
        send_halo(4 + side, col_send.at[side], col_recv.at[side], 2 + side)
    for k in range(4):
        part_k = pl.ds(0 if k < 2 else 1, 2)
        send_halo(6 + k, col_send.at[k % 2, part_k], corner_recv.at[k], 4 + k)
    send_half(e, 0, 0, to_r)
    send_half(e, 1, 3, to_l)
    for h in range(2):
        send_half(e, h, 4 + h, to_o)

    ci = lax.broadcasted_iota(jnp.int32, (8, cext), 1)
    c_lo = jnp.where(c < n_c - 1, cols + HALO, cols)
    c_hi = jnp.where(c > 0, cext - HALO, cext)
    ok_mid = (ci < c_lo) | (ci >= c_hi)
    ok_top = ok_mid & (r > 0)
    ok_bot = ok_mid & (r < n_r - 1)
    near = lane < LANES // 2
    half_d, half_a = 0.5 * diffuse_rate, 0.5 * advect_rate

    def unpack(from_right, from_left, k):
        return jnp.where(near, roll(from_right, -HALO * k, 1), roll(from_left, -HALO - HALO * k, 1))

    def fill_centre(i, ok):
        kap[i, :, 0:cols] = jnp.where(ok[:, 0:cols], half_d * jnp.exp(logk[i]), 0.0)

    def fill_outer(i, ok, from_right, from_left, k):
        outer = unpack(from_right, from_left, k)
        kap[i, :, cols:cext] = jnp.where(ok[:, cols:cext], half_d * jnp.exp(outer), 0.0)

    def fill_extra(t, ok, from_right, from_left, slot_t):
        at = slice(8 * t, 8 * t + 8)
        for p in range(3):
            scale = 1.0 if p == 0 else half_a
            outer = unpack(from_right, from_left, p * (last + 1) + slot_t)
            frame[p, at, 0:cols] = jnp.where(ok[:, 0:cols], scale * extra[p, at], 0.0)
            frame[p, at, cols:cext] = jnp.where(ok[:, cols:cext], scale * outer, 0.0)

    def coefficients(i, ok, v0, v1):
        k = kap[i]
        f_u, f_d = k + kap[i + 1], k + kap[i - 1]
        f_r, f_l = k + roll(k, -1, 1), k + roll(k, 1, 1)
        c_0[i] = jnp.where(ok, 1.0 - ((f_u + f_d) + (f_r + f_l)), 0.0)
        c_u[i] = jnp.where(ok, f_u - v0, 0.0)
        c_d[i] = jnp.where(ok, f_d + v0, 0.0)
        c_r[i] = jnp.where(ok, f_r - v1, 0.0)
        c_l[i] = jnp.where(ok, f_l + v1, 0.0)

    def step(src, i):
        u = src[i]
        return (
            c_0[i] * u
            + (c_u[i] * src[i + 1] + c_d[i] * src[i - 1])
            + (c_r[i] * roll(u, -1, 1) + c_l[i] * roll(u, 1, 1))
        )

    states = [u_0, u_1, u_2, u_3]

    for i in range(rows):
        fill_centre(HALO + i, ok_mid)
    relay_wait(0)
    wait_halo(4)
    wait_halo(5)
    for t in range(last + 1):
        fill_extra(t + 1, ok_mid, col_recv[0, 1], col_recv[1, 1], t)
    for i in range(rows):
        tile = 0 if i < per else 2
        fill_outer(HALO + i, ok_mid, col_recv[0, tile], col_recv[1, tile], i % per)

    def row_of(p, i):
        return frame[p, i + 4 : i + 5, :]

    def advance(s, i):
        new = step(states[s], i)
        if s < STEPS - 1:
            states[s + 1][i] = new
        else:
            field[8 * (i - HALO) : 8 * (i - HALO) + 8, :] = new[:, 0:cols]

    for i in range(HALO, HALO + rows):
        u_0[i] = jnp.broadcast_to(row_of(0, i), (8, cext))
    for i in range(HALO + 1, HALO + rows - 1):
        coefficients(i, ok_mid, row_of(1, i), row_of(2, i))
    relay_wait(1)
    for s in range(STEPS):
        for i in range(HALO + s + 1, HALO + rows - s - 1):
            advance(s, i)

    sens = sens_v[0]
    n_s = sens.shape[1]
    s_col = sens & (cols - 1)
    s_row = jnp.broadcast_to(sens >> (cols.bit_length() - 1), (8, n_s))
    hot_c = jnp.where(
        lax.broadcasted_iota(jnp.int32, (cols, n_s), 0) == s_col, 1.0, 0.0
    ).astype(jnp.bfloat16)

    def sensed(first_row, count, acc):
        f = field[8 * first_row : 8 * (first_row + count), :]
        f_hi, f_lo = split_bf16(f)
        f_lo2 = ((f - f_hi.astype(jnp.float32)) - f_lo.astype(jnp.float32)).astype(jnp.bfloat16)
        at = dot32(f_hi, hot_c) + (dot32(f_lo, hot_c) + dot32(f_lo2, hot_c))
        for j in range(count):
            acc = jnp.where(s_row == first_row + j, at[8 * j : 8 * j + 8], acc)
        return acc

    own = sensed(8, rows - 16, jnp.zeros((mem, n_s), jnp.float32))

    for k in (0, 1, 2, 3, 6, 7, 8, 9):
        wait_halo(k)
    fill_extra(0, ok_top, corner_recv[2, 0], corner_recv[3, 0], last)
    fill_extra(last + 2, ok_bot, corner_recv[0, 1], corner_recv[1, 1], 0)
    for k in range(HALO):
        fill_centre(k, ok_top)
        fill_outer(k, ok_top, corner_recv[2, 1], corner_recv[3, 1], per - HALO + k)
        fill_centre(HALO + rows + k, ok_bot)
        fill_outer(HALO + rows + k, ok_bot, corner_recv[0, 0], corner_recv[1, 0], k)

    for k in range(HALO):
        u_0[k] = jnp.broadcast_to(row_of(0, k), (8, cext))
        i = HALO + rows + k
        u_0[i] = jnp.broadcast_to(row_of(0, i), (8, cext))
    for i in range(1, HALO + 1):
        j = 2 * HALO + rows - 1 - i
        coefficients(i, ok_top if i < HALO else ok_mid, row_of(1, i), row_of(2, i))
        coefficients(j, ok_bot if i < HALO else ok_mid, row_of(1, j), row_of(2, j))
    for s in range(STEPS):
        for i in range(1 + s, HALO + 1 + s):
            j = 2 * HALO + rows - 1 - i
            advance(s, i)
            advance(s, j)
    own = sensed(0, 8, own)
    own = sensed(rows - 8, 8, own)
    mine = pl.ds(pl.multiple_of(e * mem, mem), mem)
    preds[mine, :] = own
    for m in range(mem):
        pred[m, 0] = own[m : m + 1]

    def spread(src, dst, ssem, rsem, ids):
        copies = []
        for d, device in enumerate(ids):
            copies.append(send(src, dst, ssem.at[d], rsem.at[d], device))
        return copies

    copies = spread(preds.at[mine], preds.at[mine], pred_ssem, pred_rsem, ens_ids)
    relay_wait(2)

    def recv_half(slot, index, h):
        remote(part(index, h), part(index, h), th_ssem.at[slot], th_rsem.at[slot], to_o).wait_recv()

    near_l, near_r, far = x_l * 2 + core, x_r * 2 + core, x_f * 2 + core
    other = x * 2 + 1 - core
    for copy in copies:
        copy.wait_recv()

    send_half(e, 1, 1, to_r)
    send_half(e, 0, 2, to_l)

    flat = preds[...]
    members = n_e * mem
    hm, qm = members // 2, members // 4
    mean = jnp.sum(flat, axis=0, keepdims=True) * (1.0 / members)
    inv_noise = 1.0 / noise_v[0]
    against = jnp.where(
        lax.broadcasted_iota(jnp.int32, (members, n_s), 0) == members - 1,
        targ_v[0] - mean, flat - mean,
    ) * inv_noise
    gram = lax.dot_general(
        preds[pl.ds(pl.multiple_of(core * hm, hm), hm), :] - mean, against,
        (((1,), (1,)), ((), ())),
        precision=lax.Precision.HIGHEST, preferred_element_type=jnp.float32,
    )
    zbuf[z] = jnp.concatenate([gram[:qm], gram[qm:]], axis=1)
    copies = spread(zbuf.at[z], zbuf.at[z], z_ssem, z_rsem, z_ids)

    def halves(index, slot):
        at = slice(slot * mem * 8, (slot + 1) * mem * 8)
        for t in range(rows // 8):
            hi, lo = split_bf16(blocks[index, :, 8 * t : 8 * t + 8, :].reshape(mem * 8, cols))
            th_hi[t, at, :] = hi
            th_lo[t, at, :] = lo

    halves(e, 0)
    recv_half(4, other, 0)
    recv_half(5, other, 1)
    halves(other, 1)
    recv_half(0, near_l, 0)
    recv_half(3, near_r, 1)
    send_half(near_l, 0, 8, to_o)
    send_half(near_r, 1, 11, to_o)
    for copy in copies:
        copy.wait_recv()

    send_half(near_l, 0, 6, to_r)
    send_half(near_r, 1, 7, to_l)
    ybuf[y] = jnp.sum(zbuf[...], axis=0)
    copies = spread(ybuf.at[y], ybuf.at[y], y_ssem, y_rsem, y_ids)
    recv_half(1, near_l, 1)
    recv_half(2, near_r, 0)
    send_half(near_l, 1, 9, to_o)
    send_half(near_r, 0, 10, to_o)
    halves(near_l, 2)
    halves(near_r, 4)
    for copy in copies:
        copy.wait_recv()
    gall[core] = jnp.sum(ybuf[...], axis=0)
    copies = [send(gall.at[core], gall.at[core], g_ssem.at[0], g_rsem.at[0], to_o)]
    for h in range(2):
        recv_half(8 + h, x_l * 2 + 1 - core, h)
        recv_half(10 + h, x_r * 2 + 1 - core, h)
    halves(x_l * 2 + 1 - core, 3)
    halves(x_r * 2 + 1 - core, 5)
    for copy in copies:
        copy.wait_recv()

    arow = lax.broadcasted_iota(jnp.int32, (members, LANES), 0)
    acol = lax.broadcasted_iota(jnp.int32, (members, LANES), 1)
    first = members + 8
    unit = (arow == acol) | ((acol >= first) & (acol < first + mem) & (acol - first == arow - e * mem))
    quarters = [gall[q][:, w : w + members] for q in range(2) for w in (0, members)]
    sums = jnp.concatenate(quarters, axis=0)
    sums = jnp.concatenate([sums, jnp.zeros_like(sums)], axis=1)
    others = jnp.sum(jnp.where(acol < members - 1, sums, 0.0), axis=1, keepdims=True)
    sums = jnp.where(
        acol == members - 1, -others,
        jnp.where(acol == members, sums[:, members - 1 : members], sums),
    )
    aug = sums * (1.0 / (members - 1)) + jnp.where(unit, 1.0, 0.0)
    aug = eliminate(aug, members, 8)
    weight = aug[:, first : first + mem] + aug[:, members : members + 1]

    wide = members * 8
    col_id = lax.broadcasted_iota(jnp.int32, (members, wide), 1)
    slots = [e, other]
    for chip in (x_l, x_r, x_f):
        slots += [chip * 2 + core, chip * 2 + 1 - core]
    k_of = (col_id // 8) % mem
    for i, index in enumerate(slots):
        k_of = jnp.where(col_id // (8 * mem) == i, k_of + index * mem, k_of)
    pick = jnp.where(lax.broadcasted_iota(jnp.int32, (members, wide), 0) == k_of, 1.0, 0.0)
    spread_w = lax.dot_general(
        weight, pick, (((0,), (0,)), ((), ())),
        precision=lax.Precision.HIGHEST, preferred_element_type=jnp.float32,
    )
    big = jnp.broadcast_to(spread_w[:, None, :], (mem, 8, wide)).reshape(mem * 8, wide)
    same = (
        lax.broadcasted_iota(jnp.int32, (mem * 8, wide), 0) % 8
        == lax.broadcasted_iota(jnp.int32, (mem * 8, wide), 1) % 8
    )
    big = jnp.where(same, big, 0.0)
    b_hi, b_lo = split_bf16(big)
    b_both = jnp.concatenate([b_hi, b_lo], axis=0)

    def product(t, lo, hi):
        two = dot32(b_both[:, lo:hi], th_hi[t, lo:hi, :])
        return two[: mem * 8] + (dot32(b_hi[:, lo:hi], th_lo[t, lo:hi, :]) + two[mem * 8 :])

    recv_half(6, far, 0)
    send_half(far, 0, 12, to_o)
    recv_half(7, far, 1)
    send_half(far, 1, 13, to_o)
    cut = wide - 2 * mem * 8
    for t in range(rows // 8):
        result[:, 8 * t : 8 * t + 8, :] = product(t, 0, cut).reshape(mem, 8, cols)
    halves(far, 6)
    recv_half(12, x_f * 2 + 1 - core, 0)
    recv_half(13, x_f * 2 + 1 - core, 1)
    halves(x_f * 2 + 1 - core, 7)
    outs = []
    for t in range(rows // 8):
        result[:, 8 * t : 8 * t + 8, :] += product(t, cut, wide).reshape(mem, 8, cols)
        copy = pltpu.make_async_copy(
            result.at[:, pl.ds(8 * t, 8)], out.at[:, pl.ds(8 * t, 8)], out_sem.at[t]
        )
        copy.start()
        outs.append(copy)
    for copy, there, _ in halo_copies:
        pl.when(there)(copy.wait_send)
    for copy in sends:
        copy.wait_send()
    for copy in outs:
        copy.wait()


def shards(sizes, theta, initial, velocity, sensors, target, noise):
    mem, rows, cols = theta.shape
    n_s = sensors.shape[-1]
    n_e, n_r, n_c, n_z = sizes
    n_y = n_r // n_z * n_c
    members = n_e * mem
    rext, cext = rows + 2 * HALO, cols + LANES
    f32 = jnp.float32
    DMA = pltpu.SemaphoreType.DMA
    return pl.pallas_call(
        functools.partial(kernel, sizes),
        out_shape=(
            jax.ShapeDtypeStruct(theta.shape, f32),
            jax.ShapeDtypeStruct((mem, 1, 1, n_s), f32),
        ),
        in_specs=[pl.BlockSpec(memory_space=pltpu.HBM)] * 6,
        out_specs=(pl.BlockSpec(memory_space=pltpu.HBM), pl.BlockSpec(memory_space=pltpu.VMEM)),
        scratch_shapes=[
            pltpu.VMEM((n_e, mem, rows, cols), f32),
            pltpu.VMEM((rext, mem, cols), f32),
            pltpu.VMEM((3, rows + 16, cols), f32),
            pltpu.VMEM((3, rows + 16, cext), f32),
            pltpu.VMEM((1, 1, n_s), jnp.int32),
            pltpu.VMEM((1, 1, n_s), f32),
            pltpu.VMEM((1, 1, n_s), f32),
            pltpu.VMEM((2, 3, 8, LANES), f32),
            pltpu.VMEM((2, 3, 8, LANES), f32),
            pltpu.VMEM((4, 2, 8, LANES), f32),
            *[pltpu.VMEM((rext, mem, cext), f32)] * 10,
            pltpu.VMEM((mem * rows, cols), f32),
            pltpu.VMEM((members, n_s), f32),
            pltpu.VMEM((n_z, members // 4, LANES), f32),
            pltpu.VMEM((n_y, members // 4, LANES), f32),
            pltpu.VMEM((2, members // 4, LANES), f32),
            pltpu.VMEM((rows // 8, members * 8, cols), jnp.bfloat16),
            pltpu.VMEM((rows // 8, members * 8, cols), jnp.bfloat16),
            pltpu.VMEM((mem, rows, cols), f32),
            DMA((6,)),
            DMA((10,)), DMA((10,)),
            DMA((n_e - 1,)), DMA((n_e - 1,)),
            DMA((n_z - 1,)), DMA((n_z - 1,)),
            DMA((n_y - 1,)), DMA((n_y - 1,)),
            DMA((1,)), DMA((1,)),
            DMA((14,)), DMA((14,)),
            DMA((rows // 8,)),
            pltpu.SemaphoreType.REGULAR((3,)),
        ],
        compiler_params=pltpu.CompilerParams(
            collective_id=0, has_side_effects=True, vmem_limit_bytes=48 * 1024 * 1024
        ),
    )(*(pltpu.with_memory_space_constraint(a, pltpu.HBM)
        for a in (theta, initial, velocity, sensors, target, noise)))


def solution(mesh):
    in_specs = (
        P("ens", "row", "col"),
        P("row", "col"),
        P(None, "row", "col"),
        P("row", "col", None),
        P("row", "col", None),
        P("row", "col", None),
    )
    out_specs = (P("ens", "row", "col"), P("ens", "row", "col", None))
    n_r = mesh.shape["row"]
    sizes = (mesh.shape["ens"], n_r, mesh.shape["col"], n_r // 2)
    return jax.shard_map(
        functools.partial(shards, sizes),
        mesh=mesh, in_specs=in_specs, out_specs=out_specs, check_vma=False,
    )
```

```python
import functools

import jax
import jax.numpy as jnp
from jax import lax
from jax.experimental import pallas as pl
from jax.experimental.pallas import tpu as pltpu
from jax.sharding import PartitionSpec as P

STEPS = 4
diffuse_rate = 0.07
advect_rate = 0.3

MESH = pl.DeviceIdType.MESH
HALO = 4
LANES = 128


def roll(x, shift, axis):
    shift = shift % x.shape[axis]
    return x if shift == 0 else pltpu.roll(x, shift, axis)


def split_bf16(x):
    hi = x.astype(jnp.bfloat16)
    lo = (x - hi.astype(jnp.float32)).astype(jnp.bfloat16)
    return hi, lo


def dot32(a, b):
    return jnp.dot(a, b, preferred_element_type=jnp.float32)


def eliminate(aug, n, p):
    arow = lax.broadcasted_iota(jnp.int32, aug.shape, 0)
    for k in range(0, n, p):
        col = [jnp.broadcast_to(aug[:, k + j : k + j + 1], aug.shape) for j in range(p)]
        d = [[col[j][k + i : k + i + 1, :] for j in range(p)] for i in range(p)]
        new = [aug[k + i : k + i + 1, :] for i in range(p)]
        for i in range(p):
            inv = 1.0 / d[i][i]
            for j in range(i + 1, p):
                d[i][j] = d[i][j] * inv
            new[i] = new[i] * inv
            for q in range(p):
                if q != i:
                    for j in range(i + 1, p):
                        d[q][j] = d[q][j] - d[q][i] * d[i][j]
                    new[q] = new[q] - d[q][i] * new[i]
        less = col[0] * new[0]
        for j in range(1, p):
            less = less + col[j] * new[j]
        aug = aug - less
        for j in range(p):
            aug = jnp.where(arow == k + j, new[j], aug)
    return aug


def kernel(
    sizes,
    theta, initial, velocity, sensors, target, noise,
    out, pred,
    blocks, logk, extra, frame, sens_v, targ_v, noise_v,
    col_send, col_recv, corner_recv,
    kap, c_0, c_u, c_d, c_r, c_l, u_0, u_1, u_2, u_3, field,
    preds, zbuf, ybuf, gall, th_hi, th_lo, result,
    load_sem, halo_ssem, halo_rsem, pred_ssem, pred_rsem,
    z_ssem, z_rsem, y_ssem, y_rsem, g_ssem, g_rsem,
    th_ssem, th_rsem, out_sem, relay_sem,
):
    n_e, n_r, n_c, n_z = sizes
    n_x = n_e // 2
    n_yh = n_r // n_z
    n_y = n_yh * n_c
    mem, rows, cols = theta.shape
    cext = cols + LANES
    e, r, c = lax.axis_index("ens"), lax.axis_index("row"), lax.axis_index("col")
    x, core = e // 2, e % 2
    yh, z = r // n_z, r % n_z
    y = yh * n_c + c

    loads = [
        pltpu.make_async_copy(theta, blocks.at[e], load_sem.at[0]),
        pltpu.make_async_copy(initial, extra.at[0, pl.ds(8, rows)], load_sem.at[1]),
        pltpu.make_async_copy(
            velocity, extra.at[pl.ds(1, 2), pl.ds(8, rows)], load_sem.at[2]
        ),
        pltpu.make_async_copy(sensors, sens_v, load_sem.at[3]),
        pltpu.make_async_copy(target, targ_v, load_sem.at[4]),
        pltpu.make_async_copy(noise, noise_v, load_sem.at[5]),
    ]
    for copy in loads:
        copy.start()

    prev, nxt = (r + n_r - 1) % n_r, (r + 1) % n_r
    left, right = (c + n_c - 1) % n_c, (c + 1) % n_c
    halo_ids = [
        {"row": prev}, {"row": nxt}, {"col": left}, {"col": right},
        {"row": prev, "col": left}, {"row": prev, "col": right},
        {"row": nxt, "col": left}, {"row": nxt, "col": right},
    ]
    ens_ids = [{"ens": (e + d) % n_e} for d in range(1, n_e)]
    z_ids = [{"row": yh * n_z + (z + d) % n_z} for d in range(1, n_z)]
    y_ids = []
    for d in range(1, n_y):
        other = (y + d) % n_y
        y_ids.append({"row": other // n_c * n_z + z, "col": other % n_c})

    has_p, has_n, has_l, has_r = r > 0, r < n_r - 1, c > 0, c < n_c - 1
    halo_out = [
        has_p, has_n, has_l, has_r, has_p & has_l, has_p & has_r, has_n & has_l, has_n & has_r
    ]
    halo_in = [
        has_n, has_p, has_r, has_l, has_n & has_r, has_n & has_l, has_p & has_r, has_p & has_l
    ]
    x_r, x_l, x_f = (x + 1) % n_x, (x + n_x - 1) % n_x, (x + 2) % n_x
    to_r, to_l = {"ens": x_r * 2 + core}, {"ens": x_l * 2 + core}
    to_o = {"ens": x * 2 + (1 - core)}
    y_r, y_l = (y + 1) % n_y, (y + n_y - 1) % n_y
    near_ids = [
        to_r, to_l, to_o,
        {"row": yh * n_z + (z + 1) % n_z}, {"row": yh * n_z + (z + n_z - 1) % n_z},
        {"row": y_r // n_c * n_z + z, "col": y_r % n_c},
        {"row": y_l // n_c * n_z + z, "col": y_l % n_c},
    ]

    barrier = pltpu.get_barrier_semaphore()
    for device in near_ids:
        pl.semaphore_signal(barrier, inc=1, device_id=device, device_id_type=MESH)
    for device, there in zip(halo_ids, halo_out, strict=True):
        @pl.when(there)
        def _(device=device):
            pl.semaphore_signal(barrier, inc=1, device_id=device, device_id_type=MESH)
    def relay_signal(j):
        for device in near_ids:
            pl.semaphore_signal(
                relay_sem.at[j], inc=1, device_id=device, device_id_type=MESH
            )

    def relay_wait(j):
        pl.semaphore_wait(relay_sem.at[j], len(near_ids))
        if j < 2:
            relay_signal(j + 1)

    sends = []

    def remote(src, dst, ssem, rsem, device):
        copy = pltpu.make_async_remote_copy(
            src_ref=src, dst_ref=dst, send_sem=ssem, recv_sem=rsem,
            device_id=device, device_id_type=MESH,
        )
        return copy

    def send(*args):
        copy = remote(*args)
        copy.start()
        sends.append(copy)
        return copy

    one = [jnp.where(v, 1, 0) for v in (has_p, has_n, has_l, has_r)]
    n_halo = (1 + one[0] + one[1]) * (1 + one[2] + one[3]) - 1
    pl.semaphore_wait(barrier, len(near_ids) + n_halo)

    relay_signal(0)

    half = mem // 2

    def part(index, h):
        return blocks.at[index, pl.ds(h * half, half)]

    def send_half(index, h, slot, device):
        return send(part(index, h), part(index, h), th_ssem.at[slot], th_rsem.at[slot], device)

    quarter = mem // 4

    def send_first(start, count, slot, device):
        here = pl.ds(start * quarter, count * quarter)
        send(theta.at[here], blocks.at[e, here], th_ssem.at[slot], th_rsem.at[slot], device)

    send_first(0, 2, 0, to_r)
    send_first(2, 2, 3, to_l)
    send_first(2, 1, 1, to_r)
    send_first(1, 1, 2, to_l)
    send_first(0, 4, 4, to_o)

    for copy in loads:
        copy.wait()

    def turned(t):
        tile = blocks[e, :, 8 * t : 8 * t + 8, :]
        logk[HALO + 8 * t : HALO + 8 * t + 8] = jnp.swapaxes(tile, 0, 1)

    last = rows // 8 - 1
    turned(0)
    turned(last)

    halo_copies = []

    def send_halo(k, src, dst, which):
        copy = remote(src, dst, halo_ssem.at[k], halo_rsem.at[k], halo_ids[which])
        pl.when(halo_out[which])(copy.start)
        halo_copies.append((copy, halo_out[which], halo_in[which]))

    def wait_halo(k):
        copy, _, there = halo_copies[k]
        pl.when(there)(copy.wait_recv)

    def edge(start):
        return logk.at[pl.ds(start, HALO)]

    def edge_x(start):
        return extra.at[:, pl.ds(start, 8)]

    for t in range(1, last):
        turned(t)

    lane = lax.broadcasted_iota(jnp.int32, (8, LANES), 1)
    slot_of = lane // HALO
    per = LANES // HALO
    for side in range(2):
        low = 0 if side == 0 else cols - LANES
        off = 0 if side == 0 else HALO
        for half_t, first_row in ((0, 0), (2, per)):
            acc = jnp.zeros((8, LANES), jnp.float32)
            for k in range(per):
                row = logk[HALO + first_row + k, :, low : low + LANES]
                acc = jnp.where(slot_of == k, roll(row, HALO * k + off, 1), acc)
            col_send[side, half_t] = acc
        acc = jnp.zeros((8, LANES), jnp.float32)
        for p in range(3):
            for t in range(last + 1):
                k = p * (last + 1) + t
                row = extra[p, 8 + 8 * t : 16 + 8 * t, low : low + LANES]
                acc = jnp.where(slot_of == k, roll(row, HALO * k + off, 1), acc)
        col_send[side, 1] = acc
    send_halo(0, edge(HALO), edge(rows + HALO), 0)
    send_halo(1, edge(rows), edge(0), 1)
    send_halo(2, edge_x(8), edge_x(rows + 8), 0)
    send_halo(3, edge_x(rows), edge_x(0), 1)
    for side in range(2):
        send_halo(4 + side, col_send.at[side], col_recv.at[side], 2 + side)
    for k in range(4):
        part_k = pl.ds(0 if k < 2 else 1, 2)
        send_halo(6 + k, col_send.at[k % 2, part_k], corner_recv.at[k], 4 + k)
    ci = lax.broadcasted_iota(jnp.int32, (8, cext), 1)
    c_lo = jnp.where(c < n_c - 1, cols + HALO, cols)
    c_hi = jnp.where(c > 0, cext - HALO, cext)
    ok_mid = (ci < c_lo) | (ci >= c_hi)
    ok_top = ok_mid & (r > 0)
    ok_bot = ok_mid & (r < n_r - 1)
    near = lane < LANES // 2
    half_d, half_a = 0.5 * diffuse_rate, 0.5 * advect_rate

    def unpack(from_right, from_left, k):
        return jnp.where(near, roll(from_right, -HALO * k, 1), roll(from_left, -HALO - HALO * k, 1))

    def fill_centre(i, ok):
        kap[i, :, 0:cols] = jnp.where(ok[:, 0:cols], half_d * jnp.exp(logk[i]), 0.0)

    def fill_outer(i, ok, from_right, from_left, k):
        outer = unpack(from_right, from_left, k)
        kap[i, :, cols:cext] = jnp.where(ok[:, cols:cext], half_d * jnp.exp(outer), 0.0)

    def fill_extra(t, ok, from_right, from_left, slot_t):
        at = slice(8 * t, 8 * t + 8)
        for p in range(3):
            scale = 1.0 if p == 0 else half_a
            outer = unpack(from_right, from_left, p * (last + 1) + slot_t)
            frame[p, at, 0:cols] = jnp.where(ok[:, 0:cols], scale * extra[p, at], 0.0)
            frame[p, at, cols:cext] = jnp.where(ok[:, cols:cext], scale * outer, 0.0)

    def coefficients(i, ok, v0, v1):
        k = kap[i]
        f_u, f_d = k + kap[i + 1], k + kap[i - 1]
        f_r, f_l = k + roll(k, -1, 1), k + roll(k, 1, 1)
        c_0[i] = jnp.where(ok, 1.0 - ((f_u + f_d) + (f_r + f_l)), 0.0)
        c_u[i] = jnp.where(ok, f_u - v0, 0.0)
        c_d[i] = jnp.where(ok, f_d + v0, 0.0)
        c_r[i] = jnp.where(ok, f_r - v1, 0.0)
        c_l[i] = jnp.where(ok, f_l + v1, 0.0)

    def step(src, i):
        u = src[i]
        return (
            c_0[i] * u
            + (c_u[i] * src[i + 1] + c_d[i] * src[i - 1])
            + (c_r[i] * roll(u, -1, 1) + c_l[i] * roll(u, 1, 1))
        )

    states = [u_0, u_1, u_2, u_3]

    for i in range(rows):
        fill_centre(HALO + i, ok_mid)
    relay_wait(0)
    wait_halo(4)
    wait_halo(5)
    for t in range(last + 1):
        fill_extra(t + 1, ok_mid, col_recv[0, 1], col_recv[1, 1], t)
    for i in range(rows):
        tile = 0 if i < per else 2
        fill_outer(HALO + i, ok_mid, col_recv[0, tile], col_recv[1, tile], i % per)

    def row_of(p, i):
        return frame[p, i + 4 : i + 5, :]

    def advance(s, i):
        new = step(states[s], i)
        if s < STEPS - 1:
            states[s + 1][i] = new
        else:
            field[8 * (i - HALO) : 8 * (i - HALO) + 8, :] = new[:, 0:cols]

    for i in range(HALO, HALO + rows):
        u_0[i] = jnp.broadcast_to(row_of(0, i), (8, cext))
    for i in range(HALO + 1, HALO + rows - 1):
        coefficients(i, ok_mid, row_of(1, i), row_of(2, i))
    relay_wait(1)
    for s in range(STEPS):
        for i in range(HALO + s + 1, HALO + rows - s - 1):
            advance(s, i)

    sens = sens_v[0]
    n_s = sens.shape[1]
    s_col = sens & (cols - 1)
    s_row = jnp.broadcast_to(sens >> (cols.bit_length() - 1), (8, n_s))
    hot_c = jnp.where(
        lax.broadcasted_iota(jnp.int32, (cols, n_s), 0) == s_col, 1.0, 0.0
    ).astype(jnp.bfloat16)

    def sensed(first_row, count, acc):
        f = field[8 * first_row : 8 * (first_row + count), :]
        f_hi, f_lo = split_bf16(f)
        f_lo2 = ((f - f_hi.astype(jnp.float32)) - f_lo.astype(jnp.float32)).astype(jnp.bfloat16)
        at = dot32(f_hi, hot_c) + (dot32(f_lo, hot_c) + dot32(f_lo2, hot_c))
        for j in range(count):
            acc = jnp.where(s_row == first_row + j, at[8 * j : 8 * j + 8], acc)
        return acc

    own = sensed(8, rows - 16, jnp.zeros((mem, n_s), jnp.float32))

    for k in (0, 1, 2, 3, 6, 7, 8, 9):
        wait_halo(k)
    fill_extra(0, ok_top, corner_recv[2, 0], corner_recv[3, 0], last)
    fill_extra(last + 2, ok_bot, corner_recv[0, 1], corner_recv[1, 1], 0)
    for k in range(HALO):
        fill_centre(k, ok_top)
        fill_outer(k, ok_top, corner_recv[2, 1], corner_recv[3, 1], per - HALO + k)
        fill_centre(HALO + rows + k, ok_bot)
        fill_outer(HALO + rows + k, ok_bot, corner_recv[0, 0], corner_recv[1, 0], k)

    for k in range(HALO):
        u_0[k] = jnp.broadcast_to(row_of(0, k), (8, cext))
        i = HALO + rows + k
        u_0[i] = jnp.broadcast_to(row_of(0, i), (8, cext))
    for i in range(1, HALO + 1):
        j = 2 * HALO + rows - 1 - i
        coefficients(i, ok_top if i < HALO else ok_mid, row_of(1, i), row_of(2, i))
        coefficients(j, ok_bot if i < HALO else ok_mid, row_of(1, j), row_of(2, j))
    for s in range(STEPS):
        for i in range(1 + s, HALO + 1 + s):
            j = 2 * HALO + rows - 1 - i
            advance(s, i)
            advance(s, j)
    own = sensed(0, 8, own)
    own = sensed(rows - 8, 8, own)
    mine = pl.ds(pl.multiple_of(e * mem, mem), mem)
    preds[mine, :] = own
    for m in range(mem):
        pred[m, 0] = own[m : m + 1]

    def spread(src, dst, ssem, rsem, ids):
        copies = []
        for d, device in enumerate(ids):
            copies.append(send(src, dst, ssem.at[d], rsem.at[d], device))
        return copies

    copies = spread(preds.at[mine], preds.at[mine], pred_ssem, pred_rsem, ens_ids)
    relay_wait(2)

    def recv_half(slot, index, h):
        remote(part(index, h), part(index, h), th_ssem.at[slot], th_rsem.at[slot], to_o).wait_recv()

    def recv_first(start, count, slot, index):
        there = blocks.at[index, pl.ds(start * quarter, count * quarter)]
        remote(there, there, th_ssem.at[slot], th_rsem.at[slot], to_o).wait_recv()

    near_l, near_r, far = x_l * 2 + core, x_r * 2 + core, x_f * 2 + core
    other = x * 2 + 1 - core
    for copy in copies:
        copy.wait_recv()

    send_first(3, 1, 5, to_r)
    send_first(0, 1, 14, to_l)
    recv_half(0, near_l, 0)
    send_half(near_l, 0, 6, to_r)
    recv_half(3, near_r, 1)
    send_half(near_r, 1, 7, to_l)

    flat = preds[...]
    members = n_e * mem
    hm, qm = members // 2, members // 4
    mean = jnp.sum(flat, axis=0, keepdims=True) * (1.0 / members)
    inv_noise = 1.0 / noise_v[0]
    against = jnp.where(
        lax.broadcasted_iota(jnp.int32, (members, n_s), 0) == members - 1,
        targ_v[0] - mean, flat - mean,
    ) * inv_noise
    gram = lax.dot_general(
        preds[pl.ds(pl.multiple_of(core * hm, hm), hm), :] - mean, against,
        (((1,), (1,)), ((), ())),
        precision=lax.Precision.HIGHEST, preferred_element_type=jnp.float32,
    )
    zbuf[z] = jnp.concatenate([gram[:qm], gram[qm:]], axis=1)
    copies = spread(zbuf.at[z], zbuf.at[z], z_ssem, z_rsem, z_ids)

    def halves(index, slot):
        at = slice(slot * mem * 8, (slot + 1) * mem * 8)
        for t in range(rows // 8):
            hi, lo = split_bf16(blocks[index, :, 8 * t : 8 * t + 8, :].reshape(mem * 8, cols))
            th_hi[t, at, :] = hi
            th_lo[t, at, :] = lo

    halves(e, 0)
    recv_first(0, 4, 4, other)
    halves(other, 1)
    send_half(near_l, 0, 8, to_o)
    send_half(near_r, 1, 11, to_o)
    for copy in copies:
        copy.wait_recv()

    ybuf[y] = jnp.sum(zbuf[...], axis=0)
    copies = spread(ybuf.at[y], ybuf.at[y], y_ssem, y_rsem, y_ids)
    recv_first(2, 1, 1, near_l)
    recv_first(3, 1, 5, near_l)
    recv_first(1, 1, 2, near_r)
    recv_first(0, 1, 14, near_r)
    send_half(near_l, 1, 9, to_o)
    send_half(near_r, 0, 10, to_o)
    halves(near_l, 2)
    halves(near_r, 4)
    for copy in copies:
        copy.wait_recv()
    gall[core] = jnp.sum(ybuf[...], axis=0)
    copies = [send(gall.at[core], gall.at[core], g_ssem.at[0], g_rsem.at[0], to_o)]
    for h in range(2):
        recv_half(8 + h, x_l * 2 + 1 - core, h)
        recv_half(10 + h, x_r * 2 + 1 - core, h)
    halves(x_l * 2 + 1 - core, 3)
    halves(x_r * 2 + 1 - core, 5)
    for copy in copies:
        copy.wait_recv()

    arow = lax.broadcasted_iota(jnp.int32, (members, LANES), 0)
    acol = lax.broadcasted_iota(jnp.int32, (members, LANES), 1)
    first = members + 8
    unit = (arow == acol) | ((acol >= first) & (acol < first + mem) & (acol - first == arow - e * mem))
    quarters = [gall[q][:, w : w + members] for q in range(2) for w in (0, members)]
    sums = jnp.concatenate(quarters, axis=0)
    sums = jnp.concatenate([sums, jnp.zeros_like(sums)], axis=1)
    others = jnp.sum(jnp.where(acol < members - 1, sums, 0.0), axis=1, keepdims=True)
    sums = jnp.where(
        acol == members - 1, -others,
        jnp.where(acol == members, sums[:, members - 1 : members], sums),
    )
    aug = sums * (1.0 / (members - 1)) + jnp.where(unit, 1.0, 0.0)
    aug = eliminate(aug, members, 8)
    weight = aug[:, first : first + mem] + aug[:, members : members + 1]

    wide = members * 8
    col_id = lax.broadcasted_iota(jnp.int32, (members, wide), 1)
    slots = [e, other]
    for chip in (x_l, x_r, x_f):
        slots += [chip * 2 + core, chip * 2 + 1 - core]
    k_of = (col_id // 8) % mem
    for i, index in enumerate(slots):
        k_of = jnp.where(col_id // (8 * mem) == i, k_of + index * mem, k_of)
    pick = jnp.where(lax.broadcasted_iota(jnp.int32, (members, wide), 0) == k_of, 1.0, 0.0)
    spread_w = lax.dot_general(
        weight, pick, (((0,), (0,)), ((), ())),
        precision=lax.Precision.HIGHEST, preferred_element_type=jnp.float32,
    )
    big = jnp.broadcast_to(spread_w[:, None, :], (mem, 8, wide)).reshape(mem * 8, wide)
    same = (
        lax.broadcasted_iota(jnp.int32, (mem * 8, wide), 0) % 8
        == lax.broadcasted_iota(jnp.int32, (mem * 8, wide), 1) % 8
    )
    big = jnp.where(same, big, 0.0)
    b_hi, b_lo = split_bf16(big)
    b_both = jnp.concatenate([b_hi, b_lo], axis=0)

    def product(t, lo, hi):
        two = dot32(b_both[:, lo:hi], th_hi[t, lo:hi, :])
        return two[: mem * 8] + (dot32(b_hi[:, lo:hi], th_lo[t, lo:hi, :]) + two[mem * 8 :])

    recv_half(6, far, 0)
    send_half(far, 0, 12, to_o)
    recv_half(7, far, 1)
    send_half(far, 1, 13, to_o)
    cut = wide - 2 * mem * 8
    for t in range(rows // 8):
        result[:, 8 * t : 8 * t + 8, :] = product(t, 0, cut).reshape(mem, 8, cols)
    halves(far, 6)
    recv_half(12, x_f * 2 + 1 - core, 0)
    recv_half(13, x_f * 2 + 1 - core, 1)
    halves(x_f * 2 + 1 - core, 7)
    outs = []
    for t in range(rows // 8):
        result[:, 8 * t : 8 * t + 8, :] += product(t, cut, wide).reshape(mem, 8, cols)
        copy = pltpu.make_async_copy(
            result.at[:, pl.ds(8 * t, 8)], out.at[:, pl.ds(8 * t, 8)], out_sem.at[t]
        )
        copy.start()
        outs.append(copy)
    for copy, there, _ in halo_copies:
        pl.when(there)(copy.wait_send)
    for copy in sends:
        copy.wait_send()
    for copy in outs:
        copy.wait()


def shards(sizes, theta, initial, velocity, sensors, target, noise):
    mem, rows, cols = theta.shape
    n_s = sensors.shape[-1]
    n_e, n_r, n_c, n_z = sizes
    n_y = n_r // n_z * n_c
    members = n_e * mem
    rext, cext = rows + 2 * HALO, cols + LANES
    f32 = jnp.float32
    DMA = pltpu.SemaphoreType.DMA
    return pl.pallas_call(
        functools.partial(kernel, sizes),
        out_shape=(
            jax.ShapeDtypeStruct(theta.shape, f32),
            jax.ShapeDtypeStruct((mem, 1, 1, n_s), f32),
        ),
        in_specs=[pl.BlockSpec(memory_space=pltpu.HBM)] * 6,
        out_specs=(pl.BlockSpec(memory_space=pltpu.HBM), pl.BlockSpec(memory_space=pltpu.VMEM)),
        scratch_shapes=[
            pltpu.VMEM((n_e, mem, rows, cols), f32),
            pltpu.VMEM((rext, mem, cols), f32),
            pltpu.VMEM((3, rows + 16, cols), f32),
            pltpu.VMEM((3, rows + 16, cext), f32),
            pltpu.VMEM((1, 1, n_s), jnp.int32),
            pltpu.VMEM((1, 1, n_s), f32),
            pltpu.VMEM((1, 1, n_s), f32),
            pltpu.VMEM((2, 3, 8, LANES), f32),
            pltpu.VMEM((2, 3, 8, LANES), f32),
            pltpu.VMEM((4, 2, 8, LANES), f32),
            *[pltpu.VMEM((rext, mem, cext), f32)] * 10,
            pltpu.VMEM((mem * rows, cols), f32),
            pltpu.VMEM((members, n_s), f32),
            pltpu.VMEM((n_z, members // 4, LANES), f32),
            pltpu.VMEM((n_y, members // 4, LANES), f32),
            pltpu.VMEM((2, members // 4, LANES), f32),
            pltpu.VMEM((rows // 8, members * 8, cols), jnp.bfloat16),
            pltpu.VMEM((rows // 8, members * 8, cols), jnp.bfloat16),
            pltpu.VMEM((mem, rows, cols), f32),
            DMA((6,)),
            DMA((10,)), DMA((10,)),
            DMA((n_e - 1,)), DMA((n_e - 1,)),
            DMA((n_z - 1,)), DMA((n_z - 1,)),
            DMA((n_y - 1,)), DMA((n_y - 1,)),
            DMA((1,)), DMA((1,)),
            DMA((15,)), DMA((15,)),
            DMA((rows // 8,)),
            pltpu.SemaphoreType.REGULAR((3,)),
        ],
        compiler_params=pltpu.CompilerParams(
            collective_id=0, has_side_effects=True, vmem_limit_bytes=48 * 1024 * 1024
        ),
    )(*(pltpu.with_memory_space_constraint(a, pltpu.HBM)
        for a in (theta, initial, velocity, sensors, target, noise)))


def solution(mesh):
    in_specs = (
        P("ens", "row", "col"),
        P("row", "col"),
        P(None, "row", "col"),
        P("row", "col", None),
        P("row", "col", None),
        P("row", "col", None),
    )
    out_specs = (P("ens", "row", "col"), P("ens", "row", "col", None))
    n_r = mesh.shape["row"]
    sizes = (mesh.shape["ens"], n_r, mesh.shape["col"], n_r // 2)
    return jax.shard_map(
        functools.partial(shards, sizes),
        mesh=mesh, in_specs=in_specs, out_specs=out_specs, check_vma=False,
    )
```

```python
import functools

import jax
import jax.numpy as jnp
from jax import lax
from jax.experimental import pallas as pl
from jax.experimental.pallas import tpu as pltpu
from jax.sharding import PartitionSpec as P

STEPS = 4
diffuse_rate = 0.07
advect_rate = 0.3

MESH = pl.DeviceIdType.MESH
HALO = 4
LANES = 128


def roll(x, shift, axis):
    shift = shift % x.shape[axis]
    return x if shift == 0 else pltpu.roll(x, shift, axis)


def split_bf16(x):
    hi = x.astype(jnp.bfloat16)
    lo = (x - hi.astype(jnp.float32)).astype(jnp.bfloat16)
    return hi, lo


def dot32(a, b):
    return jnp.dot(a, b, preferred_element_type=jnp.float32)


def eliminate(aug, n, p):
    arow = lax.broadcasted_iota(jnp.int32, aug.shape, 0)
    for k in range(0, n, p):
        col = [jnp.broadcast_to(aug[:, k + j : k + j + 1], aug.shape) for j in range(p)]
        d = [[col[j][k + i : k + i + 1, :] for j in range(p)] for i in range(p)]
        new = [aug[k + i : k + i + 1, :] for i in range(p)]
        for i in range(p):
            inv = 1.0 / d[i][i]
            for j in range(i + 1, p):
                d[i][j] = d[i][j] * inv
            new[i] = new[i] * inv
            for q in range(p):
                if q != i:
                    for j in range(i + 1, p):
                        d[q][j] = d[q][j] - d[q][i] * d[i][j]
                    new[q] = new[q] - d[q][i] * new[i]
        less = col[0] * new[0]
        for j in range(1, p):
            less = less + col[j] * new[j]
        aug = aug - less
        for j in range(p):
            aug = jnp.where(arow == k + j, new[j], aug)
    return aug


def kernel(
    sizes,
    theta, initial, velocity, sensors, target, noise,
    out, pred,
    blocks, logk, extra, frame, sens_v, targ_v, noise_v,
    col_send, col_recv, corner_recv,
    kap, c_0, c_u, c_d, c_r, c_l, u_0, u_1, u_2, u_3, field,
    preds, zbuf, ybuf, gall, th_hi, th_lo, result,
    load_sem, halo_ssem, halo_rsem, pred_ssem, pred_rsem,
    z_ssem, z_rsem, y_ssem, y_rsem, g_ssem, g_rsem,
    th_ssem, th_rsem, out_sem, relay_sem,
):
    n_e, n_r, n_c, n_z = sizes
    n_x = n_e // 2
    n_yh = n_r // n_z
    n_y = n_yh * n_c
    mem, rows, cols = theta.shape
    cext = cols + LANES
    e, r, c = lax.axis_index("ens"), lax.axis_index("row"), lax.axis_index("col")
    x, core = e // 2, e % 2
    yh, z = r // n_z, r % n_z
    y = yh * n_c + c

    loads = [
        pltpu.make_async_copy(theta, blocks.at[e], load_sem.at[0]),
        pltpu.make_async_copy(initial, extra.at[0, pl.ds(8, rows)], load_sem.at[1]),
        pltpu.make_async_copy(
            velocity, extra.at[pl.ds(1, 2), pl.ds(8, rows)], load_sem.at[2]
        ),
        pltpu.make_async_copy(sensors, sens_v, load_sem.at[3]),
        pltpu.make_async_copy(target, targ_v, load_sem.at[4]),
        pltpu.make_async_copy(noise, noise_v, load_sem.at[5]),
    ]
    for copy in loads:
        copy.start()

    prev, nxt = (r + n_r - 1) % n_r, (r + 1) % n_r
    left, right = (c + n_c - 1) % n_c, (c + 1) % n_c
    halo_ids = [
        {"row": prev}, {"row": nxt}, {"col": left}, {"col": right},
        {"row": prev, "col": left}, {"row": prev, "col": right},
        {"row": nxt, "col": left}, {"row": nxt, "col": right},
    ]
    ens_ids = [{"ens": (e + d) % n_e} for d in range(1, n_e)]
    z_ids = [{"row": yh * n_z + (z + d) % n_z} for d in range(1, n_z)]
    y_ids = []
    for d in range(1, n_y):
        other = (y + d) % n_y
        y_ids.append({"row": other // n_c * n_z + z, "col": other % n_c})

    has_p, has_n, has_l, has_r = r > 0, r < n_r - 1, c > 0, c < n_c - 1
    halo_out = [
        has_p, has_n, has_l, has_r, has_p & has_l, has_p & has_r, has_n & has_l, has_n & has_r
    ]
    halo_in = [
        has_n, has_p, has_r, has_l, has_n & has_r, has_n & has_l, has_p & has_r, has_p & has_l
    ]
    x_r, x_l, x_f = (x + 1) % n_x, (x + n_x - 1) % n_x, (x + 2) % n_x
    to_r, to_l = {"ens": x_r * 2 + core}, {"ens": x_l * 2 + core}
    to_o = {"ens": x * 2 + (1 - core)}
    y_r, y_l = (y + 1) % n_y, (y + n_y - 1) % n_y
    near_ids = [
        to_r, to_l, to_o,
        {"row": yh * n_z + (z + 1) % n_z}, {"row": yh * n_z + (z + n_z - 1) % n_z},
        {"row": y_r // n_c * n_z + z, "col": y_r % n_c},
        {"row": y_l // n_c * n_z + z, "col": y_l % n_c},
    ]

    barrier = pltpu.get_barrier_semaphore()
    for device in near_ids:
        pl.semaphore_signal(barrier, inc=1, device_id=device, device_id_type=MESH)
    for device, there in zip(halo_ids, halo_out, strict=True):
        @pl.when(there)
        def _(device=device):
            pl.semaphore_signal(barrier, inc=1, device_id=device, device_id_type=MESH)
    def relay_signal(j):
        for device in near_ids:
            pl.semaphore_signal(
                relay_sem.at[j], inc=1, device_id=device, device_id_type=MESH
            )

    def relay_wait(j):
        pl.semaphore_wait(relay_sem.at[j], len(near_ids))
        if j < 2:
            relay_signal(j + 1)

    sends = []

    def remote(src, dst, ssem, rsem, device):
        copy = pltpu.make_async_remote_copy(
            src_ref=src, dst_ref=dst, send_sem=ssem, recv_sem=rsem,
            device_id=device, device_id_type=MESH,
        )
        return copy

    def send(*args):
        copy = remote(*args)
        copy.start()
        sends.append(copy)
        return copy

    one = [jnp.where(v, 1, 0) for v in (has_p, has_n, has_l, has_r)]
    n_halo = (1 + one[0] + one[1]) * (1 + one[2] + one[3]) - 1
    pl.semaphore_wait(barrier, len(near_ids) + n_halo)

    relay_signal(0)

    half = mem // 2

    def part(index, h):
        return blocks.at[index, pl.ds(h * half, half)]

    def send_half(index, h, slot, device):
        return send(part(index, h), part(index, h), th_ssem.at[slot], th_rsem.at[slot], device)

    quarter = mem // 4

    def send_first(start, count, slot, device):
        here = pl.ds(start * quarter, count * quarter)
        send(theta.at[here], blocks.at[e, here], th_ssem.at[slot], th_rsem.at[slot], device)

    send_first(0, 2, 0, to_r)
    send_first(2, 2, 3, to_l)
    send_first(2, 1, 1, to_r)
    send_first(1, 1, 2, to_l)
    send_first(0, 4, 4, to_o)

    for copy in loads:
        copy.wait()

    def turned(t):
        tile = blocks[e, :, 8 * t : 8 * t + 8, :]
        logk[HALO + 8 * t : HALO + 8 * t + 8] = jnp.swapaxes(tile, 0, 1)

    last = rows // 8 - 1
    turned(0)
    turned(last)

    halo_copies = []

    def send_halo(k, src, dst, which):
        copy = remote(src, dst, halo_ssem.at[k], halo_rsem.at[k], halo_ids[which])
        pl.when(halo_out[which])(copy.start)
        halo_copies.append((copy, halo_out[which], halo_in[which]))

    def wait_halo(k):
        copy, _, there = halo_copies[k]
        pl.when(there)(copy.wait_recv)

    def edge(start):
        return logk.at[pl.ds(start, HALO)]

    def edge_x(start):
        return extra.at[:, pl.ds(start, 8)]

    for t in range(1, last):
        turned(t)

    lane = lax.broadcasted_iota(jnp.int32, (8, LANES), 1)
    slot_of = lane // HALO
    per = LANES // HALO
    for side in range(2):
        low = 0 if side == 0 else cols - LANES
        off = 0 if side == 0 else HALO
        for half_t, first_row in ((0, 0), (2, per)):
            acc = jnp.zeros((8, LANES), jnp.float32)
            for k in range(per):
                row = logk[HALO + first_row + k, :, low : low + LANES]
                acc = jnp.where(slot_of == k, roll(row, HALO * k + off, 1), acc)
            col_send[side, half_t] = acc
        acc = jnp.zeros((8, LANES), jnp.float32)
        for p in range(3):
            for t in range(last + 1):
                k = p * (last + 1) + t
                row = extra[p, 8 + 8 * t : 16 + 8 * t, low : low + LANES]
                acc = jnp.where(slot_of == k, roll(row, HALO * k + off, 1), acc)
        col_send[side, 1] = acc
    send_halo(0, edge(HALO), edge(rows + HALO), 0)
    send_halo(1, edge(rows), edge(0), 1)
    send_halo(2, edge_x(8), edge_x(rows + 8), 0)
    send_halo(3, edge_x(rows), edge_x(0), 1)
    for side in range(2):
        send_halo(4 + side, col_send.at[side], col_recv.at[side], 2 + side)
    for k in range(4):
        part_k = pl.ds(0 if k < 2 else 1, 2)
        send_halo(6 + k, col_send.at[k % 2, part_k], corner_recv.at[k], 4 + k)
    ci = lax.broadcasted_iota(jnp.int32, (8, cext), 1)
    c_lo = jnp.where(c < n_c - 1, cols + HALO, cols)
    c_hi = jnp.where(c > 0, cext - HALO, cext)
    ok_mid = (ci < c_lo) | (ci >= c_hi)
    ok_top = ok_mid & (r > 0)
    ok_bot = ok_mid & (r < n_r - 1)
    near = lane < LANES // 2
    half_d, half_a = 0.5 * diffuse_rate, 0.5 * advect_rate

    def unpack(from_right, from_left, k):
        return jnp.where(near, roll(from_right, -HALO * k, 1), roll(from_left, -HALO - HALO * k, 1))

    def fill_centre(i, ok):
        kap[i, :, 0:cols] = jnp.where(ok[:, 0:cols], half_d * jnp.exp(logk[i]), 0.0)

    def fill_outer(i, ok, from_right, from_left, k):
        outer = unpack(from_right, from_left, k)
        kap[i, :, cols:cext] = jnp.where(ok[:, cols:cext], half_d * jnp.exp(outer), 0.0)

    def fill_extra(t, ok, from_right, from_left, slot_t):
        at = slice(8 * t, 8 * t + 8)
        for p in range(3):
            scale = 1.0 if p == 0 else half_a
            outer = unpack(from_right, from_left, p * (last + 1) + slot_t)
            frame[p, at, 0:cols] = jnp.where(ok[:, 0:cols], scale * extra[p, at], 0.0)
            frame[p, at, cols:cext] = jnp.where(ok[:, cols:cext], scale * outer, 0.0)

    def coefficients(i, ok, v0, v1):
        k = kap[i]
        f_u, f_d = k + kap[i + 1], k + kap[i - 1]
        f_r, f_l = k + roll(k, -1, 1), k + roll(k, 1, 1)
        c_0[i] = jnp.where(ok, 1.0 - ((f_u + f_d) + (f_r + f_l)), 0.0)
        c_u[i] = jnp.where(ok, f_u - v0, 0.0)
        c_d[i] = jnp.where(ok, f_d + v0, 0.0)
        c_r[i] = jnp.where(ok, f_r - v1, 0.0)
        c_l[i] = jnp.where(ok, f_l + v1, 0.0)

    def step(src, i):
        u = src[i]
        return (
            c_0[i] * u
            + (c_u[i] * src[i + 1] + c_d[i] * src[i - 1])
            + (c_r[i] * roll(u, -1, 1) + c_l[i] * roll(u, 1, 1))
        )

    states = [u_0, u_1, u_2, u_3]

    for i in range(rows):
        fill_centre(HALO + i, ok_mid)
    relay_wait(0)
    wait_halo(4)
    wait_halo(5)
    for t in range(last + 1):
        fill_extra(t + 1, ok_mid, col_recv[0, 1], col_recv[1, 1], t)
    for i in range(rows):
        tile = 0 if i < per else 2
        fill_outer(HALO + i, ok_mid, col_recv[0, tile], col_recv[1, tile], i % per)

    def row_of(p, i):
        return frame[p, i + 4 : i + 5, :]

    def advance(s, i):
        new = step(states[s], i)
        if s < STEPS - 1:
            states[s + 1][i] = new
        else:
            field[8 * (i - HALO) : 8 * (i - HALO) + 8, :] = new[:, 0:cols]

    for i in range(HALO, HALO + rows):
        u_0[i] = jnp.broadcast_to(row_of(0, i), (8, cext))
    for i in range(HALO + 1, HALO + rows - 1):
        coefficients(i, ok_mid, row_of(1, i), row_of(2, i))
    relay_wait(1)
    for s in range(STEPS):
        for i in range(HALO + s + 1, HALO + rows - s - 1):
            advance(s, i)

    sens = sens_v[0]
    n_s = sens.shape[1]
    s_col = sens & (cols - 1)
    s_row = jnp.broadcast_to(sens >> (cols.bit_length() - 1), (8, n_s))
    hot_c = jnp.where(
        lax.broadcasted_iota(jnp.int32, (cols, n_s), 0) == s_col, 1.0, 0.0
    ).astype(jnp.bfloat16)

    def sensed(first_row, count, acc):
        f = field[8 * first_row : 8 * (first_row + count), :]
        f_hi, f_lo = split_bf16(f)
        f_lo2 = ((f - f_hi.astype(jnp.float32)) - f_lo.astype(jnp.float32)).astype(jnp.bfloat16)
        at = dot32(f_hi, hot_c) + (dot32(f_lo, hot_c) + dot32(f_lo2, hot_c))
        for j in range(count):
            acc = jnp.where(s_row == first_row + j, at[8 * j : 8 * j + 8], acc)
        return acc

    own = sensed(8, rows - 16, jnp.zeros((mem, n_s), jnp.float32))

    for k in (0, 1, 2, 3, 6, 7, 8, 9):
        wait_halo(k)
    fill_extra(0, ok_top, corner_recv[2, 0], corner_recv[3, 0], last)
    fill_extra(last + 2, ok_bot, corner_recv[0, 1], corner_recv[1, 1], 0)
    for k in range(HALO):
        fill_centre(k, ok_top)
        fill_outer(k, ok_top, corner_recv[2, 1], corner_recv[3, 1], per - HALO + k)
        fill_centre(HALO + rows + k, ok_bot)
        fill_outer(HALO + rows + k, ok_bot, corner_recv[0, 0], corner_recv[1, 0], k)

    for k in range(HALO):
        u_0[k] = jnp.broadcast_to(row_of(0, k), (8, cext))
        i = HALO + rows + k
        u_0[i] = jnp.broadcast_to(row_of(0, i), (8, cext))
    for i in range(1, HALO + 1):
        j = 2 * HALO + rows - 1 - i
        coefficients(i, ok_top if i < HALO else ok_mid, row_of(1, i), row_of(2, i))
        coefficients(j, ok_bot if i < HALO else ok_mid, row_of(1, j), row_of(2, j))
    for s in range(STEPS):
        for i in range(1 + s, HALO + 1 + s):
            j = 2 * HALO + rows - 1 - i
            advance(s, i)
            advance(s, j)
    own = sensed(0, 8, own)
    own = sensed(rows - 8, 8, own)
    mine = pl.ds(pl.multiple_of(e * mem, mem), mem)
    preds[mine, :] = own
    for m in range(mem):
        pred[m, 0] = own[m : m + 1]

    def spread(src, dst, ssem, rsem, ids):
        copies = []
        for d, device in enumerate(ids):
            copies.append(send(src, dst, ssem.at[d], rsem.at[d], device))
        return copies

    copies = spread(preds.at[mine], preds.at[mine], pred_ssem, pred_rsem, ens_ids)
    relay_wait(2)

    def recv_half(slot, index, h):
        remote(part(index, h), part(index, h), th_ssem.at[slot], th_rsem.at[slot], to_o).wait_recv()

    def recv_first(start, count, slot, index):
        there = blocks.at[index, pl.ds(start * quarter, count * quarter)]
        remote(there, there, th_ssem.at[slot], th_rsem.at[slot], to_o).wait_recv()

    near_l, near_r, far = x_l * 2 + core, x_r * 2 + core, x_f * 2 + core
    other = x * 2 + 1 - core
    for copy in copies:
        copy.wait_recv()

    send_first(3, 1, 5, to_r)
    send_first(0, 1, 14, to_l)

    flat = preds[...]
    members = n_e * mem
    hm, qm = members // 2, members // 4
    mean = jnp.sum(flat, axis=0, keepdims=True) * (1.0 / members)
    inv_noise = 1.0 / noise_v[0]
    against = jnp.where(
        lax.broadcasted_iota(jnp.int32, (members, n_s), 0) == members - 1,
        targ_v[0] - mean, flat - mean,
    ) * inv_noise
    gram = lax.dot_general(
        preds[pl.ds(pl.multiple_of(core * hm, hm), hm), :] - mean, against,
        (((1,), (1,)), ((), ())),
        precision=lax.Precision.HIGHEST, preferred_element_type=jnp.float32,
    )
    zbuf[z] = jnp.concatenate([gram[:qm], gram[qm:]], axis=1)
    copies = spread(zbuf.at[z], zbuf.at[z], z_ssem, z_rsem, z_ids)
    recv_half(0, near_l, 0)
    send_half(near_l, 0, 6, to_r)
    recv_half(3, near_r, 1)
    send_half(near_r, 1, 7, to_l)

    def halves(index, slot):
        at = slice(slot * mem * 8, (slot + 1) * mem * 8)
        for t in range(rows // 8):
            hi, lo = split_bf16(blocks[index, :, 8 * t : 8 * t + 8, :].reshape(mem * 8, cols))
            th_hi[t, at, :] = hi
            th_lo[t, at, :] = lo

    halves(e, 0)
    recv_first(0, 4, 4, other)
    halves(other, 1)
    send_half(near_l, 0, 8, to_o)
    send_half(near_r, 1, 11, to_o)
    for copy in copies:
        copy.wait_recv()

    ybuf[y] = jnp.sum(zbuf[...], axis=0)
    copies = spread(ybuf.at[y], ybuf.at[y], y_ssem, y_rsem, y_ids)
    recv_first(2, 1, 1, near_l)
    recv_first(3, 1, 5, near_l)
    recv_first(1, 1, 2, near_r)
    recv_first(0, 1, 14, near_r)
    send_half(near_l, 1, 9, to_o)
    send_half(near_r, 0, 10, to_o)
    halves(near_l, 2)
    halves(near_r, 4)
    for copy in copies:
        copy.wait_recv()
    gall[core] = jnp.sum(ybuf[...], axis=0)
    copies = [send(gall.at[core], gall.at[core], g_ssem.at[0], g_rsem.at[0], to_o)]
    for h in range(2):
        recv_half(8 + h, x_l * 2 + 1 - core, h)
        recv_half(10 + h, x_r * 2 + 1 - core, h)
    halves(x_l * 2 + 1 - core, 3)
    halves(x_r * 2 + 1 - core, 5)
    for copy in copies:
        copy.wait_recv()

    arow = lax.broadcasted_iota(jnp.int32, (members, LANES), 0)
    acol = lax.broadcasted_iota(jnp.int32, (members, LANES), 1)
    first = members + 8
    unit = (arow == acol) | ((acol >= first) & (acol < first + mem) & (acol - first == arow - e * mem))
    quarters = [gall[q][:, w : w + members] for q in range(2) for w in (0, members)]
    sums = jnp.concatenate(quarters, axis=0)
    sums = jnp.concatenate([sums, jnp.zeros_like(sums)], axis=1)
    others = jnp.sum(jnp.where(acol < members - 1, sums, 0.0), axis=1, keepdims=True)
    sums = jnp.where(
        acol == members - 1, -others,
        jnp.where(acol == members, sums[:, members - 1 : members], sums),
    )
    aug = sums * (1.0 / (members - 1)) + jnp.where(unit, 1.0, 0.0)
    aug = eliminate(aug, members, 8)
    weight = aug[:, first : first + mem] + aug[:, members : members + 1]

    wide = members * 8
    col_id = lax.broadcasted_iota(jnp.int32, (members, wide), 1)
    slots = [e, other]
    for chip in (x_l, x_r, x_f):
        slots += [chip * 2 + core, chip * 2 + 1 - core]
    k_of = (col_id // 8) % mem
    for i, index in enumerate(slots):
        k_of = jnp.where(col_id // (8 * mem) == i, k_of + index * mem, k_of)
    pick = jnp.where(lax.broadcasted_iota(jnp.int32, (members, wide), 0) == k_of, 1.0, 0.0)
    spread_w = lax.dot_general(
        weight, pick, (((0,), (0,)), ((), ())),
        precision=lax.Precision.HIGHEST, preferred_element_type=jnp.float32,
    )
    big = jnp.broadcast_to(spread_w[:, None, :], (mem, 8, wide)).reshape(mem * 8, wide)
    same = (
        lax.broadcasted_iota(jnp.int32, (mem * 8, wide), 0) % 8
        == lax.broadcasted_iota(jnp.int32, (mem * 8, wide), 1) % 8
    )
    big = jnp.where(same, big, 0.0)
    b_hi, b_lo = split_bf16(big)
    b_both = jnp.concatenate([b_hi, b_lo], axis=0)

    def product(t, lo, hi):
        two = dot32(b_both[:, lo:hi], th_hi[t, lo:hi, :])
        return two[: mem * 8] + (dot32(b_hi[:, lo:hi], th_lo[t, lo:hi, :]) + two[mem * 8 :])

    recv_half(6, far, 0)
    send_half(far, 0, 12, to_o)
    recv_half(7, far, 1)
    send_half(far, 1, 13, to_o)
    cut = wide - 2 * mem * 8
    for t in range(rows // 8):
        result[:, 8 * t : 8 * t + 8, :] = product(t, 0, cut).reshape(mem, 8, cols)
    halves(far, 6)
    recv_half(12, x_f * 2 + 1 - core, 0)
    recv_half(13, x_f * 2 + 1 - core, 1)
    halves(x_f * 2 + 1 - core, 7)
    outs = []
    for t in range(rows // 8):
        result[:, 8 * t : 8 * t + 8, :] += product(t, cut, wide).reshape(mem, 8, cols)
        copy = pltpu.make_async_copy(
            result.at[:, pl.ds(8 * t, 8)], out.at[:, pl.ds(8 * t, 8)], out_sem.at[t]
        )
        copy.start()
        outs.append(copy)
    for copy, there, _ in halo_copies:
        pl.when(there)(copy.wait_send)
    for copy in sends:
        copy.wait_send()
    for copy in outs:
        copy.wait()


def shards(sizes, theta, initial, velocity, sensors, target, noise):
    mem, rows, cols = theta.shape
    n_s = sensors.shape[-1]
    n_e, n_r, n_c, n_z = sizes
    n_y = n_r // n_z * n_c
    members = n_e * mem
    rext, cext = rows + 2 * HALO, cols + LANES
    f32 = jnp.float32
    DMA = pltpu.SemaphoreType.DMA
    return pl.pallas_call(
        functools.partial(kernel, sizes),
        out_shape=(
            jax.ShapeDtypeStruct(theta.shape, f32),
            jax.ShapeDtypeStruct((mem, 1, 1, n_s), f32),
        ),
        in_specs=[pl.BlockSpec(memory_space=pltpu.HBM)] * 6,
        out_specs=(pl.BlockSpec(memory_space=pltpu.HBM), pl.BlockSpec(memory_space=pltpu.VMEM)),
        scratch_shapes=[
            pltpu.VMEM((n_e, mem, rows, cols), f32),
            pltpu.VMEM((rext, mem, cols), f32),
            pltpu.VMEM((3, rows + 16, cols), f32),
            pltpu.VMEM((3, rows + 16, cext), f32),
            pltpu.VMEM((1, 1, n_s), jnp.int32),
            pltpu.VMEM((1, 1, n_s), f32),
            pltpu.VMEM((1, 1, n_s), f32),
            pltpu.VMEM((2, 3, 8, LANES), f32),
            pltpu.VMEM((2, 3, 8, LANES), f32),
            pltpu.VMEM((4, 2, 8, LANES), f32),
            *[pltpu.VMEM((rext, mem, cext), f32)] * 10,
            pltpu.VMEM((mem * rows, cols), f32),
            pltpu.VMEM((members, n_s), f32),
            pltpu.VMEM((n_z, members // 4, LANES), f32),
            pltpu.VMEM((n_y, members // 4, LANES), f32),
            pltpu.VMEM((2, members // 4, LANES), f32),
            pltpu.VMEM((rows // 8, members * 8, cols), jnp.bfloat16),
            pltpu.VMEM((rows // 8, members * 8, cols), jnp.bfloat16),
            pltpu.VMEM((mem, rows, cols), f32),
            DMA((6,)),
            DMA((10,)), DMA((10,)),
            DMA((n_e - 1,)), DMA((n_e - 1,)),
            DMA((n_z - 1,)), DMA((n_z - 1,)),
            DMA((n_y - 1,)), DMA((n_y - 1,)),
            DMA((1,)), DMA((1,)),
            DMA((15,)), DMA((15,)),
            DMA((rows // 8,)),
            pltpu.SemaphoreType.REGULAR((3,)),
        ],
        compiler_params=pltpu.CompilerParams(
            collective_id=0, has_side_effects=True, vmem_limit_bytes=48 * 1024 * 1024
        ),
    )(*(pltpu.with_memory_space_constraint(a, pltpu.HBM)
        for a in (theta, initial, velocity, sensors, target, noise)))


def solution(mesh):
    in_specs = (
        P("ens", "row", "col"),
        P("row", "col"),
        P(None, "row", "col"),
        P("row", "col", None),
        P("row", "col", None),
        P("row", "col", None),
    )
    out_specs = (P("ens", "row", "col"), P("ens", "row", "col", None))
    n_r = mesh.shape["row"]
    sizes = (mesh.shape["ens"], n_r, mesh.shape["col"], n_r // 2)
    return jax.shard_map(
        functools.partial(shards, sizes),
        mesh=mesh, in_specs=in_specs, out_specs=out_specs, check_vma=False,
    )
```
